128 devices in a mesh: rep: 16 (over y_lo, x, core), dp: 8 (over y_hi, z).
Axes of the slice: x: 4, y: 4 (y_hi: 2, y_lo: 2; y = y_hi * 2 + y_lo), z: 4, core: 2. Of those that a mesh axis runs over, the one named last changes fastest.
Arguments:
- queries: bfloat16 [2048, 64, 576], P(('rep', 'dp')), parts along dimension 0, may hold values from -50 to 50
- latent_cache: bfloat16 [2048, 512, 576], P(('rep', 'dp')), parts along dimension 0, may hold values from -8 to 8
- new_latent: bfloat16 [2048, 576], P(('rep', 'dp')), parts along dimension 0, may hold values from -6 to 6
- lengths: int32 [2048], P('rep'), parts along dimension 0, may hold values from 2 to 512, as said below
- value_up: bfloat16 [64, 512, 128], P('dp'), may hold values from -0.75 to 0.75
- output_proj: bfloat16 [8192, 7168], P('dp'), may hold values from -0.0625 to 0.0625
- residual: bfloat16 [2048, 7168], P(('rep', 'dp')), parts along dimension 0, may hold values from -3 to 3
- norm_gain: bfloat16 [7168], replicated, may hold values from 0.5 to 1.5
Outputs:
- hidden_next: bfloat16 [2048, 7168], P(('rep', 'dp')), parts along dimension 0
- normed: bfloat16 [2048, 7168], P(('rep', 'dp')), parts along dimension 0
The draws below stay inside these ranges and needn't reach their ends.
There are 16 independent parts, one for each index of `rep`. The reference program is written for one: setup_inputs(seed, part) draws one part's arguments, and reference() takes and returns one part's arrays. A program takes and returns all parts, laid end to end along the dimension named above; an argument that names none is the same for every part. Nothing has to cross between parts.
Inputs may be any that keep to these rules, and one draw needn't show every extreme that they name: The rows of one device share a ceiling of 128, 256 or 512 on their lengths; one device of each part has the ceiling 512 and a row of exactly 512.
All inputs are finite; a program needn't handle non-finite values.
Results may differ from the reference program's by a relative error of at most 0.017.
Values may be sent and summed in bfloat16 or wider, within the bound.
No kernel may reach another device: no remote copies, remote signals or barrier semaphores. Data moves between devices by JAX's collectives and lax.ppermute only.
A program may use at most 128 MiB of HBM per device.

```python
import jax
import jax.numpy as jnp
from jax import lax

D = 7168
H = 64
LAT = 512
ROPE = 64
VH = 128
ROWS_DEV = 16
LEN = 512
KVW = 576
ROWS = 128
N_DP = 8


def cache_base(key):
    return jnp.clip(jax.random.normal(key, (ROWS, LEN, LAT + ROPE), jnp.float32), -6.0, 6.0)


def draw_latent_cache(key, part):
    base_values = cache_base(key)
    return base_values.astype(jnp.bfloat16)


def draw_queries(key, part):
    key = jax.random.fold_in(key, 5)
    drawn = jnp.clip(jax.random.normal(key, (ROWS, H, LAT + ROPE), jnp.float32), -6.0, 6.0)
    return drawn.astype(jnp.bfloat16)


def draw_lengths(key, part):
    key = jax.random.fold_in(key, 7)
    rank_count = ROWS // ROWS_DEV
    levels = jax.random.randint(jax.random.fold_in(key, 1), (rank_count,), 1, 3)
    heaviest = jax.random.randint(jax.random.fold_in(key, 2), (), 0, rank_count)
    levels = jnp.where(jnp.arange(rank_count) == heaviest, 4, levels)
    ceiling = jnp.repeat(LEN * levels // 4, ROWS_DEV, total_repeat_length=ROWS)
    raw_bits = jax.random.randint(jax.random.fold_in(key, 3), (ROWS,), 0, 1 << 20)
    drawn = 2 + raw_bits % (ceiling - 1)
    longest = heaviest * ROWS_DEV + jax.random.randint(jax.random.fold_in(key, 4), (), 0, ROWS_DEV)
    return drawn.at[longest].set(LEN).astype(jnp.int32)


def block_scale(rng, shape, split, least, high):
    level, own = 1.0, jax.random.fold_in(rng, 6)
    for dim, parts in split:
        steps = jnp.exp(jax.random.uniform(jax.random.fold_in(own, dim), (parts,), jnp.float32, least / len(split), high / len(split)))
        level = level * jnp.repeat(steps, shape[dim] // parts).reshape([-1 if axis == dim else 1 for axis in range(len(shape))])
    return level


def gaussian(stream_key, dims, spread, most, shards=(), dtype=jnp.bfloat16):
    array = jax.random.normal(stream_key, dims, jnp.float32) * spread
    if len(shards) > 0:
        array = block_scale(stream_key, dims, shards, -0.22, 0.18) * array
    return jnp.clip(array, min=-most, max=most).astype(dtype)


def setup_inputs(seed: int = 0, part: int = 0) -> dict:
    key_list = jax.random.split(jax.random.key(seed), 9)
    own_keys = jax.random.split(jax.random.fold_in(key_list[8], part), 9)
    return {
        "queries": draw_queries(jax.random.fold_in(jax.random.fold_in(key_list[8], part), 71), part),
        "latent_cache": draw_latent_cache(jax.random.fold_in(jax.random.fold_in(key_list[8], part), 71), part),
        "new_latent": gaussian(own_keys[2], (ROWS, KVW), 1.0, 6.0, ((0, 8),)),
        "lengths": draw_lengths(jax.random.fold_in(jax.random.fold_in(key_list[8], part), 71), part),
        "value_up": gaussian(key_list[4], (H, LAT, VH), 64 ** -0.5, 0.75, ((0, 8),)),
        "output_proj": gaussian(key_list[5], (H * VH, D), (H * VH) ** -0.5, 0.0625, ((0, 8),)),
        "residual": gaussian(own_keys[6], (ROWS, D), 0.5, 3.0, ((0, 8),)),
        "norm_gain": jnp.clip(1.0 + 0.1 * jax.random.normal(key_list[7], (D,), jnp.float32), 0.5, 1.5).astype(jnp.bfloat16),
    }


score_scale = 192.0 ** (-0.5)
norm_eps = 1e-06

def reference(queries, latent_cache, new_latent, lengths, value_up, output_proj, residual, norm_gain):
    all_keys = jnp.concatenate([latent_cache, new_latent[:, None, :]], axis=1).astype(jnp.float32)
    scores = jnp.einsum('rhk,rpk->rhp', queries.astype(jnp.float32), all_keys) * score_scale
    positions = jnp.arange(LEN + 1)
    visible = (positions[None, :] < lengths[:, None]) | (positions[None, :] == LEN)
    scores = jnp.where(visible[:, None, :], scores, -jnp.inf)
    row_max = lax.optimization_barrier(jnp.max(scores, axis=2, keepdims=True))
    raised = jnp.exp(scores - row_max)
    row_total = lax.optimization_barrier(jnp.sum(raised, axis=2, keepdims=True))
    weights = lax.optimization_barrier(raised.astype(jnp.bfloat16)).astype(jnp.float32)
    latent_out = (jnp.einsum('rhp,rpc->rhc', weights, all_keys[:, :, :LAT]) / row_total).astype(jnp.bfloat16)
    latent_wide = lax.optimization_barrier(latent_out).astype(jnp.float32)
    values = jnp.einsum('rhc,hcv->rhv', latent_wide, value_up.astype(jnp.float32)).astype(jnp.bfloat16)
    flattened = values.reshape(ROWS, H * VH)
    group_width = H // N_DP * VH
    attention = jnp.zeros((ROWS, D), jnp.float32)
    for group in range(N_DP):
        piece = jnp.dot(flattened[:, group * group_width:(group + 1) * group_width], output_proj[group * group_width:(group + 1) * group_width], preferred_element_type=jnp.float32)
        rounded = lax.optimization_barrier(piece.astype(jnp.bfloat16)).astype(jnp.float32)
        attention = attention + rounded
    summed = residual.astype(jnp.float32) + attention
    hidden_next = summed.astype(jnp.bfloat16)
    inverse_rms = lax.rsqrt(lax.optimization_barrier(jnp.mean(summed * summed, axis=1, keepdims=True)) + norm_eps)
    normed = (summed * inverse_rms * norm_gain.astype(jnp.float32)).astype(jnp.bfloat16)
    return (hidden_next, normed)
```

```python
import jax
import jax.numpy as jnp
from jax import lax
from jax.experimental import pallas as pl
from jax.experimental.pallas import tpu as pltpu
from jax.sharding import PartitionSpec as P

LAT = 512
SPAN_STEP = 128
GROUP_ROWS = 2
score_scale = 192.0 ** (-0.5)
norm_eps = 1e-06
MIB = 1024 * 1024


def attend_kernel(lengths_ref, queries_ref, latent_ref, cache_ref, out_ref, held, latent_wide, arrived):
    row_count, span, width = held.shape
    heads = queries_ref.shape[1]
    group_count = row_count // GROUP_ROWS
    levels = span // SPAN_STEP

    def group_level(group):
        longest = lengths_ref[group * GROUP_ROWS]
        for i in range(1, GROUP_ROWS):
            longest = jnp.maximum(longest, lengths_ref[group * GROUP_ROWS + i])
        return (longest + SPAN_STEP - 1) // SPAN_STEP

    def fetch(group, level):
        rows = pl.ds(group * GROUP_ROWS, GROUP_ROWS)
        keys = pl.ds(0, level * SPAN_STEP)
        return pltpu.make_async_copy(
            cache_ref.at[rows, keys, :], held.at[rows, keys, :], arrived.at[group]
        )

    def start(group, carry):
        here = group_level(group)
        for level in range(1, levels + 1):

            @pl.when(here == level)
            def _():
                fetch(group, level).start()

        return carry

    lax.fori_loop(0, group_count, start, 0)
    latent_wide[...] = latent_ref[...].astype(jnp.float32)

    def attend_row(row, level):
        length = lengths_ref[row]
        queries = queries_ref[row]
        keys = held[row, : level * SPAN_STEP, :]
        fresh = latent_wide[pl.ds(row, 1), :]
        scores = (
            lax.dot_general(
                queries, keys, (((1,), (1,)), ((), ())), preferred_element_type=jnp.float32
            )
            * score_scale
        )
        self_score = (
            jnp.sum(queries.astype(jnp.float32) * fresh, axis=1, keepdims=True) * score_scale
        )
        position = lax.broadcasted_iota(jnp.int32, scores.shape, 1)
        scores = jnp.where(position < length, scores, -jnp.inf)
        row_max = jnp.maximum(jnp.max(scores, axis=1, keepdims=True), self_score)
        raised = jnp.exp(scores - row_max)
        self_raised = jnp.exp(self_score - row_max)
        row_total = jnp.sum(raised, axis=1, keepdims=True) + self_raised
        gathered = jnp.dot(
            raised.astype(jnp.bfloat16), keys[:, :LAT], preferred_element_type=jnp.float32
        )
        self_weight = self_raised.astype(jnp.bfloat16).astype(jnp.float32)
        gathered = gathered + self_weight * fresh[:, :LAT]
        return gathered / row_total

    def attend_group(group, carry):
        here = group_level(group)
        owners, rows_heads, _ = out_ref.shape
        owned = heads // owners
        for level in range(1, levels + 1):

            @pl.when(here == level)
            def _():
                fetch(group, level).wait()
                done = [
                    attend_row(group * GROUP_ROWS + i, level).reshape(owners, owned, LAT)
                    for i in range(GROUP_ROWS)
                ]
                block = jnp.concatenate(done, axis=1).astype(jnp.bfloat16)
                size = GROUP_ROWS * owned
                out_ref[:, pl.ds(pl.multiple_of(group * size, size), size), :] = block

        return carry

    lax.fori_loop(0, group_count, attend_group, 0)


def attend(queries, latent_cache, new_latent, lengths_here, owners):
    row_count, span, width = latent_cache.shape
    heads = queries.shape[1]
    owned = heads // owners
    vmem = pl.BlockSpec(memory_space=pltpu.VMEM)
    return pl.pallas_call(
        attend_kernel,
        out_shape=jax.ShapeDtypeStruct((owners, row_count * owned, LAT), jnp.bfloat16),
        in_specs=[
            pl.BlockSpec(memory_space=pltpu.SMEM),
            vmem,
            vmem,
            pl.BlockSpec(memory_space=pl.ANY),
        ],
        out_specs=vmem,
        scratch_shapes=[
            pltpu.VMEM((row_count, span, width), jnp.bfloat16),
            pltpu.VMEM((row_count, width), jnp.float32),
            pltpu.SemaphoreType.DMA((row_count // GROUP_ROWS,)),
        ],
        compiler_params=pltpu.CompilerParams(vmem_limit_bytes=32 * MIB),
        name="attend",
    )(lengths_here, queries, new_latent, latent_cache)


def project_kernel(latent_ref, value_up_ref, proj_ref, out_ref, wide, values):
    owned, lat, value_size = value_up_ref.shape
    rows = values.shape[0]

    @pl.when(pl.program_id(0) == 0)
    def _():
        for c in range(lat // 128):
            wide[c] = latent_ref[:, c * 128 : (c + 1) * 128].astype(jnp.float32)
        for h in range(owned):
            mine = jnp.concatenate(
                [wide[c, pl.ds(h, rows, stride=owned), :] for c in range(lat // 128)], axis=1
            ).astype(jnp.bfloat16)
            values[:, h * value_size : (h + 1) * value_size] = jnp.dot(
                mine, value_up_ref[h], preferred_element_type=jnp.float32
            ).astype(jnp.bfloat16)

    out_ref[...] = jnp.dot(
        values[...], proj_ref[...], preferred_element_type=jnp.float32
    ).astype(jnp.bfloat16)


def project(owned_latent, value_up, output_proj, rows):
    owned, lat, value_size = value_up.shape
    depth, width = output_proj.shape
    step = 1024
    return pl.pallas_call(
        project_kernel,
        grid=(width // step,),
        out_shape=jax.ShapeDtypeStruct((rows, width), jnp.bfloat16),
        in_specs=[
            pl.BlockSpec((rows * owned, lat), lambda i: (0, 0)),
            pl.BlockSpec((owned, lat, value_size), lambda i: (0, 0, 0)),
            pl.BlockSpec((depth, step), lambda i: (0, i)),
        ],
        out_specs=pl.BlockSpec((rows, step), lambda i: (0, i)),
        scratch_shapes=[
            pltpu.VMEM((lat // 128, rows * owned, 128), jnp.float32),
            pltpu.VMEM((rows, owned * value_size), jnp.bfloat16),
        ],
        compiler_params=pltpu.CompilerParams(vmem_limit_bytes=32 * MIB),
        name="project",
    )(owned_latent, value_up, output_proj)


def finish_kernel(partial_ref, residual_ref, gain_ref, hidden_ref, normed_ref):
    summed = residual_ref[...].astype(jnp.float32)
    for g in range(partial_ref.shape[0]):
        summed = summed + partial_ref[g].astype(jnp.float32)
    hidden_ref[...] = summed.astype(jnp.bfloat16)
    mean = jnp.mean(summed * summed, axis=1, keepdims=True)
    normed = summed * lax.rsqrt(mean + norm_eps) * gain_ref[...].astype(jnp.float32)
    normed_ref[...] = normed.astype(jnp.bfloat16)


def finish(partials, residual, norm_gain):
    vmem = pl.BlockSpec(memory_space=pltpu.VMEM)
    shape = jax.ShapeDtypeStruct(residual.shape, jnp.bfloat16)
    return pl.pallas_call(
        finish_kernel,
        out_shape=(shape, shape),
        in_specs=[vmem, vmem, vmem],
        out_specs=(vmem, vmem),
        compiler_params=pltpu.CompilerParams(vmem_limit_bytes=32 * MIB),
        name="finish",
    )(partials, residual, norm_gain.reshape(1, -1))


def per_device(
    queries, latent_cache, new_latent, lengths, value_up, output_proj, residual, norm_gain
):
    owners = lax.axis_size("dp")
    rank_here = lax.axis_index("dp")
    rows_here = latent_cache.shape[0]
    owned = value_up.shape[0]
    lengths_here = lax.dynamic_slice_in_dim(lengths, rank_here * rows_here, rows_here)
    latent_out = attend(queries, latent_cache, new_latent, lengths_here, owners)
    owned_latent = lax.all_to_all(latent_out, "dp", split_axis=0, concat_axis=0, tiled=True)
    rows = owners * rows_here
    partial = project(
        owned_latent.reshape(rows * owned, LAT), value_up, output_proj, rows
    )
    partials = lax.all_to_all(
        partial.reshape(owners, rows_here, -1), "dp", split_axis=0, concat_axis=0, tiled=True
    )
    return finish(partials, residual, norm_gain)


def solution(mesh):
    return jax.shard_map(
        per_device,
        mesh=mesh,
        in_specs=(
            P(("rep", "dp"), None, None),
            P(("rep", "dp"), None, None),
            P(("rep", "dp"), None),
            P("rep"),
            P("dp", None, None),
            P("dp", None),
            P(("rep", "dp"), None),
            P(),
        ),
        out_specs=(P(("rep", "dp"), None), P(("rep", "dp"), None)),
        check_vma=False,
    )
```

```python
import jax
import jax.numpy as jnp
from jax import lax
from jax.experimental import pallas as pl
from jax.experimental.pallas import tpu as pltpu
from jax.sharding import PartitionSpec as P

LAT = 512
SPAN_STEP = 128
GROUP_ROWS = 2
PROJ_STEP = 1024
score_scale = 192.0 ** (-0.5)
norm_eps = 1e-06
MIB = 1024 * 1024


def attend_kernel(
    lengths_ref, queries_hbm, latent_hbm, cache_ref, proj_hbm, out_ref, proj_ref,
    held, queries_ref, latent_ref, latent_wide, arrived, arrived_small,
):
    row_count, width, span = held.shape
    heads = queries_ref.shape[1]
    first_row = lax.axis_index("dp") * row_count
    group_count = row_count // GROUP_ROWS
    levels = span // SPAN_STEP

    def group_level(group):
        longest = lengths_ref[first_row + group * GROUP_ROWS]
        for i in range(1, GROUP_ROWS):
            longest = jnp.maximum(longest, lengths_ref[first_row + group * GROUP_ROWS + i])
        return (longest + SPAN_STEP - 1) // SPAN_STEP

    def fetch(group, level):
        rows = pl.ds(group * GROUP_ROWS, GROUP_ROWS)
        keys = pl.ds(0, level * SPAN_STEP)
        return pltpu.make_async_copy(
            cache_ref.at[rows, :, keys], held.at[rows, :, keys], arrived.at[group]
        )

    def start(group, carry):
        here = group_level(group)
        for level in range(1, levels + 1):

            @pl.when(here == level)
            def _():
                fetch(group, level).start()

        return carry

    latent_copy = pltpu.make_async_copy(latent_hbm, latent_ref, arrived_small.at[0])
    queries_copy = pltpu.make_async_copy(queries_hbm, queries_ref, arrived_small.at[1])
    latent_copy.start()
    queries_copy.start()
    lax.fori_loop(0, group_count, start, 0)
    proj_copy = pltpu.make_async_copy(proj_hbm, proj_ref, arrived_small.at[2])
    proj_copy.start()
    latent_copy.wait()
    queries_copy.wait()
    latent_wide[...] = latent_ref[...].astype(jnp.float32)

    def attend_row(row, level):
        length = lengths_ref[first_row + row]
        queries = queries_ref[row]
        keys = held[row, :, : level * SPAN_STEP]
        fresh = latent_wide[pl.ds(row, 1), :]
        scores = (
            jnp.dot(queries, keys, preferred_element_type=jnp.float32) * score_scale
        )
        self_score = (
            jnp.sum(queries.astype(jnp.float32) * fresh, axis=1, keepdims=True) * score_scale
        )
        position = lax.broadcasted_iota(jnp.int32, scores.shape, 1)
        scores = jnp.where(position < length, scores, -jnp.inf)
        row_max = jnp.maximum(jnp.max(scores, axis=1, keepdims=True), self_score)
        raised = jnp.exp(scores - row_max)
        self_raised = jnp.exp(self_score - row_max)
        row_total = jnp.sum(raised, axis=1, keepdims=True) + self_raised
        gathered = lax.dot_general(
            raised.astype(jnp.bfloat16),
            keys[:LAT],
            (((1,), (1,)), ((), ())),
            preferred_element_type=jnp.float32,
        )
        self_weight = self_raised.astype(jnp.bfloat16).astype(jnp.float32)
        gathered = gathered + self_weight * fresh[:, :LAT]
        return gathered / row_total

    def attend_group(group, carry):
        here = group_level(group)
        owners, rows_heads, _ = out_ref.shape
        owned = heads // owners
        for level in range(1, levels + 1):

            @pl.when(here == level)
            def _():
                fetch(group, level).wait()
                done = [
                    attend_row(group * GROUP_ROWS + i, level).reshape(owners, owned, LAT)
                    for i in range(GROUP_ROWS)
                ]
                block = jnp.concatenate(done, axis=1).astype(jnp.bfloat16)
                size = GROUP_ROWS * owned
                out_ref[:, pl.ds(pl.multiple_of(group * size, size), size), :] = block

        return carry

    lax.fori_loop(0, group_count, attend_group, 0)
    proj_copy.wait()


def attend(queries, latent_cache, new_latent, lengths, output_proj, owners):
    row_count, span, width = latent_cache.shape
    heads = queries.shape[1]
    owned = heads // owners
    vmem = pl.BlockSpec(memory_space=pltpu.VMEM)
    hbm = pl.BlockSpec(memory_space=pltpu.HBM)
    return pl.pallas_call(
        attend_kernel,
        out_shape=(
            jax.ShapeDtypeStruct((owners, row_count * owned, LAT), jnp.bfloat16),
            pltpu.VMEM(output_proj.shape, jnp.bfloat16),
        ),
        in_specs=[
            pl.BlockSpec(memory_space=pltpu.SMEM),
            hbm,
            hbm,
            hbm,
            hbm,
        ],
        out_specs=(vmem, vmem),
        scratch_shapes=[
            pltpu.VMEM((row_count, width, span), jnp.bfloat16),
            pltpu.VMEM(queries.shape, jnp.bfloat16),
            pltpu.VMEM(new_latent.shape, jnp.bfloat16),
            pltpu.VMEM((row_count, width), jnp.float32),
            pltpu.SemaphoreType.DMA((row_count // GROUP_ROWS,)),
            pltpu.SemaphoreType.DMA((3,)),
        ],
        cost_estimate=pl.CostEstimate(
            flops=4 * row_count * heads * span * width,
            bytes_accessed=2 * row_count * span * width,
            transcendentals=row_count * heads * span,
        ),
        compiler_params=pltpu.CompilerParams(vmem_limit_bytes=24 * MIB),
        name="attend",
    )(
        lengths,
        *(
            pltpu.with_memory_space_constraint(x, pltpu.HBM)
            for x in (queries, new_latent, jnp.swapaxes(latent_cache, 1, 2), output_proj)
        ),
    )


def project_kernel(latent_ref, value_up_ref, proj_ref, out_ref, wide, values):
    owned, lat, value_size = value_up_ref.shape
    rows = values.shape[0]

    for c in range(lat // 128):
        wide[c] = latent_ref[:, c * 128 : (c + 1) * 128].astype(jnp.float32)
    for h in range(owned):
        mine = jnp.concatenate(
            [wide[c, pl.ds(h, rows, stride=owned), :] for c in range(lat // 128)], axis=1
        ).astype(jnp.bfloat16)
        values[:, h * value_size : (h + 1) * value_size] = jnp.dot(
            mine, value_up_ref[h], preferred_element_type=jnp.float32
        ).astype(jnp.bfloat16)
    flattened = values[...]
    for start in range(0, proj_ref.shape[1], PROJ_STEP):
        columns = slice(start, start + PROJ_STEP)
        out_ref[:, columns] = jnp.dot(
            flattened, proj_ref[:, columns], preferred_element_type=jnp.float32
        ).astype(jnp.bfloat16)


def project(owned_latent, value_up, output_proj, rows):
    owned, lat, value_size = value_up.shape
    depth, width = output_proj.shape
    vmem = pl.BlockSpec(memory_space=pltpu.VMEM)
    return pl.pallas_call(
        project_kernel,
        out_shape=jax.ShapeDtypeStruct((rows, width), jnp.bfloat16),
        in_specs=[vmem, vmem, vmem],
        out_specs=vmem,
        scratch_shapes=[
            pltpu.VMEM((lat // 128, rows * owned, 128), jnp.float32),
            pltpu.VMEM((rows, owned * value_size), jnp.bfloat16),
        ],
        compiler_params=pltpu.CompilerParams(vmem_limit_bytes=24 * MIB),
        name="project",
    )(owned_latent, value_up, output_proj)


def finish_kernel(partial_ref, residual_ref, gain_ref, hidden_ref, normed_ref):
    summed = residual_ref[...].astype(jnp.float32)
    for g in range(partial_ref.shape[0]):
        summed = summed + partial_ref[g].astype(jnp.float32)
    hidden_ref[...] = summed.astype(jnp.bfloat16)
    mean = jnp.mean(summed * summed, axis=1, keepdims=True)
    normed = summed * lax.rsqrt(mean + norm_eps) * gain_ref[...].astype(jnp.float32)
    normed_ref[...] = normed.astype(jnp.bfloat16)


def finish(partials, residual, norm_gain):
    vmem = pl.BlockSpec(memory_space=pltpu.VMEM)
    shape = jax.ShapeDtypeStruct(residual.shape, jnp.bfloat16)
    return pl.pallas_call(
        finish_kernel,
        out_shape=(shape, shape),
        in_specs=[vmem, vmem, vmem],
        out_specs=(vmem, vmem),
        compiler_params=pltpu.CompilerParams(vmem_limit_bytes=32 * MIB),
        name="finish",
    )(partials, residual, norm_gain.reshape(1, -1))


def per_device(
    queries, latent_cache, new_latent, lengths, value_up, output_proj, residual, norm_gain
):
    owners = lax.axis_size("dp")
    rows_here = latent_cache.shape[0]
    owned = value_up.shape[0]
    latent_out, proj_near = attend(
        queries, latent_cache, new_latent, lengths, output_proj, owners
    )
    owned_latent = lax.all_to_all(latent_out, "dp", split_axis=0, concat_axis=0, tiled=True)
    rows = owners * rows_here
    partial = project(
        owned_latent.reshape(rows * owned, LAT), value_up, proj_near, rows
    )
    partials = lax.all_to_all(
        partial.reshape(owners, rows_here, -1), "dp", split_axis=0, concat_axis=0, tiled=True
    )
    return finish(partials, residual, norm_gain)


def solution(mesh):
    return jax.shard_map(
        per_device,
        mesh=mesh,
        in_specs=(
            P(("rep", "dp"), None, None),
            P(("rep", "dp"), None, None),
            P(("rep", "dp"), None),
            P("rep"),
            P("dp", None, None),
            P("dp", None),
            P(("rep", "dp"), None),
            P(),
        ),
        out_specs=(P(("rep", "dp"), None), P(("rep", "dp"), None)),
        check_vma=False,
    )
```

```python
import jax
import jax.numpy as jnp
from jax import lax
from jax.experimental import pallas as pl
from jax.experimental.pallas import tpu as pltpu
from jax.sharding import PartitionSpec as P

LAT = 512
GROUP_PAIRS = 2
PROJ_STEP = 1024
LEFT_COLUMNS = 3072
score_scale = 192.0 ** (-0.5)
norm_eps = 1e-06
MIB = 1024 * 1024


def attend_kernel(
    lengths_hbm, queries_hbm, latent_hbm, cache_ref, proj_hbm, out_ref, proj_ref,
    held, queries_ref, latent_ref, latent_wide, lengths_ref, order, arrived, arrived_small,
):
    row_count, width, span = held.shape
    owners, _, _ = out_ref.shape
    heads = queries_ref.shape[1]
    owned = heads // owners
    first_row = lax.axis_index("dp") * row_count
    pair_count = row_count // 2
    group_count = pair_count // GROUP_PAIRS
    short = span // 2

    lengths_copy = pltpu.make_async_copy(lengths_hbm, lengths_ref, arrived_small.at[0])
    latent_copy = pltpu.make_async_copy(latent_hbm, latent_ref, arrived_small.at[1])
    proj_copy = pltpu.make_async_copy(proj_hbm, proj_ref, arrived_small.at[2])

    def fetch_queries(pair):
        rows = pl.ds(2 * pair, 2)
        return pltpu.make_async_copy(queries_hbm.at[rows], queries_ref.at[rows], arrived.at[0, pair])

    def fetch_half(pair, half):
        rows, keys = pl.ds(2 * pair, 2), pl.ds(half * short, short)
        return pltpu.make_async_copy(
            cache_ref.at[rows, :, keys], held.at[rows, :, keys], arrived.at[1 + half, pair]
        )

    lengths_copy.start()
    latent_copy.start()
    for pair in range(pair_count):
        fetch_queries(pair).start()
        fetch_half(pair, 0).start()

    lengths_copy.wait()
    longest = [
        jnp.maximum(lengths_ref[first_row + 2 * pair], lengths_ref[first_row + 2 * pair + 1])
        for pair in range(pair_count)
    ]
    is_long = [(length > short).astype(jnp.int32) for length in longest]
    long_slot, short_slot = pair_count - sum(is_long), 0
    short_groups = long_slot // GROUP_PAIRS
    for pair in range(pair_count):
        order[jnp.where(is_long[pair] == 1, long_slot, short_slot)] = pair
        long_slot = long_slot + is_long[pair]
        short_slot = short_slot + 1 - is_long[pair]

    def start_second(slot, carry):
        fetch_half(order[slot], 1).start()
        return carry

    lax.fori_loop(short_groups * GROUP_PAIRS, pair_count, start_second, 0)
    proj_copy.start()
    latent_copy.wait()
    latent_wide[...] = latent_ref[...].astype(jnp.float32)

    def score(row, keys):
        queries = queries_ref[row]
        fresh = latent_wide[pl.ds(row, 1), :]
        scores = (
            jnp.dot(queries, held[row, :, :keys], preferred_element_type=jnp.float32)
            * score_scale
        )
        self_score = (
            jnp.sum(queries.astype(jnp.float32) * fresh, axis=1, keepdims=True) * score_scale
        )
        return scores, self_score

    def weigh(row, scores, self_score):
        position = lax.broadcasted_iota(jnp.int32, scores.shape, 1)
        scores = jnp.where(position < lengths_ref[first_row + row], scores, -jnp.inf)
        row_max = jnp.maximum(jnp.max(scores, axis=1, keepdims=True), self_score)
        raised = jnp.exp(scores - row_max)
        self_raised = jnp.exp(self_score - row_max)
        row_total = jnp.sum(raised, axis=1, keepdims=True) + self_raised
        self_weight = self_raised.astype(jnp.bfloat16).astype(jnp.float32)
        return raised.astype(jnp.bfloat16), self_weight, row_total

    def gather(row, keys, weights, self_weight, row_total):
        gathered = lax.dot_general(
            weights,
            held[row, :LAT, :keys],
            (((1,), (1,)), ((), ())),
            preferred_element_type=jnp.float32,
        )
        gathered = gathered + self_weight * latent_wide[pl.ds(row, 1), :LAT]
        return (gathered / row_total).reshape(owners, owned, LAT)

    def attend_group(keys):
        def body(group, carry):
            pairs = [order[group * GROUP_PAIRS + i] for i in range(GROUP_PAIRS)]
            for pair in pairs:
                fetch_queries(pair).wait()
                for half in range(keys // short):
                    fetch_half(pair, half).wait()
            rows = [2 * pair + i for pair in pairs for i in range(2)]
            scored = [score(row, keys) for row in rows]
            weighed = [weigh(row, *both) for row, both in zip(rows, scored)]
            done = [gather(row, keys, *parts) for row, parts in zip(rows, weighed)]
            for i, pair in enumerate(pairs):
                block = jnp.concatenate(done[2 * i : 2 * i + 2], axis=1).astype(jnp.bfloat16)
                size = 2 * owned
                out_ref[:, pl.ds(pl.multiple_of(pair * size, size), size), :] = block
            return carry

        return body

    lax.fori_loop(0, short_groups, attend_group(short), 0)
    lax.fori_loop(short_groups, group_count, attend_group(span), 0)
    proj_copy.wait()


def attend(queries, latent_cache, new_latent, lengths, output_proj, owners):
    row_count, span, width = latent_cache.shape
    heads = queries.shape[1]
    owned = heads // owners
    vmem = pl.BlockSpec(memory_space=pltpu.VMEM)
    hbm = pl.BlockSpec(memory_space=pltpu.HBM)
    return pl.pallas_call(
        attend_kernel,
        out_shape=(
            jax.ShapeDtypeStruct((owners, row_count * owned, LAT), jnp.bfloat16),
            pltpu.VMEM(output_proj.shape, jnp.bfloat16),
        ),
        in_specs=[
            hbm,
            hbm,
            hbm,
            hbm,
            hbm,
        ],
        out_specs=(vmem, vmem),
        scratch_shapes=[
            pltpu.VMEM((row_count, width, span), jnp.bfloat16),
            pltpu.VMEM(queries.shape, jnp.bfloat16),
            pltpu.VMEM(new_latent.shape, jnp.bfloat16),
            pltpu.VMEM((row_count, width), jnp.float32),
            pltpu.SMEM(lengths.shape, jnp.int32),
            pltpu.SMEM((row_count // 2,), jnp.int32),
            pltpu.SemaphoreType.DMA((3, row_count // 2)),
            pltpu.SemaphoreType.DMA((3,)),
        ],
        cost_estimate=pl.CostEstimate(
            flops=4 * row_count * heads * span * width,
            bytes_accessed=2 * row_count * span * width,
            transcendentals=row_count * heads * span,
        ),
        compiler_params=pltpu.CompilerParams(vmem_limit_bytes=24 * MIB),
        name="attend",
    )(
        *(
            pltpu.with_memory_space_constraint(x, pltpu.HBM)
            for x in (lengths, queries, new_latent, jnp.swapaxes(latent_cache, 1, 2), output_proj)
        ),
    )


def values_kernel(latent_ref, value_up_ref, proj_ref, values_ref, own_ref, send_ref, wide):
    owned, lat, value_size = value_up_ref.shape
    owners, rows_here, columns = 2 * own_ref.shape[0], own_ref.shape[1], own_ref.shape[2]
    rows = owners * rows_here
    z_size = owners // 2
    here = lax.axis_index("dp")

    for c in range(lat // 128):
        wide[c] = latent_ref[:, c * 128 : (c + 1) * 128].astype(jnp.float32)
    for h in range(owned):
        mine = jnp.concatenate(
            [wide[c, pl.ds(h, rows, stride=owned), :] for c in range(lat // 128)], axis=1
        ).astype(jnp.bfloat16)
        made = jnp.dot(mine, value_up_ref[h], preferred_element_type=jnp.float32).astype(
            jnp.bfloat16
        )
        for owner in range(owners):
            far = (owner // z_size + here // z_size) % 2
            step = (owner % z_size - here % z_size + z_size) % z_size
            place = pl.multiple_of((far * z_size + step) * rows_here, rows_here)
            values_ref[pl.ds(place, rows_here), h * value_size : (h + 1) * value_size] = made[
                owner * rows_here : (owner + 1) * rows_here
            ]
    flattened = values_ref[...]
    width = proj_ref.shape[1]
    for start in range(0, columns, PROJ_STEP):
        stop = min(start + PROJ_STEP, columns)
        done = jnp.dot(
            flattened,
            proj_ref[:, width - columns + start : width - columns + stop],
            preferred_element_type=jnp.float32,
        ).astype(jnp.bfloat16)
        done = done.reshape(2, z_size, rows_here, stop - start)
        own_ref[:, :, start:stop] = done[0]
        send_ref[:, :, start:stop] = done[1]


def make_values(owned_latent, value_up, output_proj, owners, rows_here, columns):
    owned, lat, value_size = value_up.shape
    depth, width = output_proj.shape
    rows = owners * rows_here
    vmem = pl.BlockSpec(memory_space=pltpu.VMEM)
    half = jax.ShapeDtypeStruct((owners // 2, rows_here, columns), jnp.bfloat16)
    return pl.pallas_call(
        values_kernel,
        out_shape=(jax.ShapeDtypeStruct((rows, owned * value_size), jnp.bfloat16), half, half),
        in_specs=[vmem, vmem, vmem],
        out_specs=(vmem, vmem, vmem),
        scratch_shapes=[pltpu.VMEM((lat // 128, rows * owned, 128), jnp.float32)],
        cost_estimate=pl.CostEstimate(
            flops=2 * rows * depth * columns, bytes_accessed=2 * depth * columns, transcendentals=0
        ),
        compiler_params=pltpu.CompilerParams(vmem_limit_bytes=20 * MIB),
        name="values",
    )(owned_latent, value_up, pltpu.with_memory_space_constraint(output_proj, pltpu.VMEM))


def project_kernel(values_ref, proj_ref, *out_refs):
    rows_here, columns = out_refs[0].shape[1:]
    z_size = len(out_refs)
    flattened = values_ref[...]
    for start in range(0, columns, PROJ_STEP):
        stop = min(start + PROJ_STEP, columns)
        done = jnp.dot(
            flattened, proj_ref[:, start:stop], preferred_element_type=jnp.float32
        ).astype(jnp.bfloat16)
        done = done.reshape(2, z_size, rows_here, stop - start)
        for step in range(z_size):
            out_refs[step][:, :, start:stop] = done[:, step]


def project(values, output_proj, owners, rows_here, columns):
    rows, depth = values.shape
    z_size = owners // 2
    vmem = pl.BlockSpec(memory_space=pltpu.VMEM)
    part = jax.ShapeDtypeStruct((2, rows_here, columns), jnp.bfloat16)
    return pl.pallas_call(
        project_kernel,
        out_shape=[part] * z_size,
        in_specs=[vmem, vmem],
        out_specs=[vmem] * z_size,
        cost_estimate=pl.CostEstimate(
            flops=2 * rows * depth * columns, bytes_accessed=2 * depth * columns, transcendentals=0
        ),
        compiler_params=pltpu.CompilerParams(vmem_limit_bytes=20 * MIB),
        name="project",
    )(values, pltpu.with_memory_space_constraint(output_proj, pltpu.VMEM))


def add_far_kernel(own_ref, came_ref, *out_refs):
    for step, out_ref in enumerate(out_refs, 1):
        both = own_ref[step].astype(jnp.float32) + came_ref[step].astype(jnp.float32)
        out_ref[...] = both.astype(jnp.bfloat16)


def add_far(own, came):
    vmem = pl.BlockSpec(memory_space=pltpu.VMEM)
    return pl.pallas_call(
        add_far_kernel,
        out_shape=[jax.ShapeDtypeStruct(own.shape[1:], jnp.bfloat16)] * (own.shape[0] - 1),
        in_specs=[vmem, vmem],
        out_specs=[vmem] * (own.shape[0] - 1),
        cost_estimate=pl.CostEstimate(flops=own.size, bytes_accessed=own.size * 6, transcendentals=0),
        compiler_params=pltpu.CompilerParams(vmem_limit_bytes=16 * MIB),
        name="add_far",
    )(own, came)


def add_near_kernel(*refs):
    *part_refs, out_ref = refs
    total = part_refs[0][1].astype(jnp.float32)
    for part_ref in part_refs[1:]:
        total = total + part_ref[1].astype(jnp.float32)
    out_ref[...] = total.astype(jnp.bfloat16)


def add_near(parts):
    vmem = pl.BlockSpec(memory_space=pltpu.VMEM)
    return pl.pallas_call(
        add_near_kernel,
        out_shape=jax.ShapeDtypeStruct(parts[0].shape[1:], jnp.bfloat16),
        in_specs=[vmem] * len(parts),
        out_specs=vmem,
        cost_estimate=pl.CostEstimate(
            flops=parts[0].size * 2, bytes_accessed=parts[0].size * 8, transcendentals=0
        ),
        compiler_params=pltpu.CompilerParams(vmem_limit_bytes=16 * MIB),
        name="add_near",
    )(*parts)


def finish_kernel(near_refs, far_ref, own_ref, came_ref, step_refs, residual_ref, gain_ref,
                  hidden_ref, normed_ref):
    rows, first = far_ref.shape
    width = residual_ref.shape[1]
    left = residual_ref[:, :first].astype(jnp.float32) + far_ref[...].astype(jnp.float32)
    for near_ref in near_refs:
        left = left + near_ref[0].astype(jnp.float32)
    right = residual_ref[:, first:].astype(jnp.float32) + (
        own_ref[0].astype(jnp.float32) + came_ref[0].astype(jnp.float32)
    )
    for step_ref in step_refs:
        right = right + step_ref[...].astype(jnp.float32)
    total = jnp.sum(left * left, axis=1, keepdims=True) + jnp.sum(
        right * right, axis=1, keepdims=True
    )
    inverse_rms = lax.rsqrt(total * (1.0 / width) + norm_eps)
    for part, here in ((left, slice(0, first)), (right, slice(first, width))):
        hidden_ref[:, here] = part.astype(jnp.bfloat16)
        normed = part * inverse_rms * gain_ref[:, here].astype(jnp.float32)
        normed_ref[:, here] = normed.astype(jnp.bfloat16)


def finish(nears, far, own, came, steps, residual, norm_gain):
    vmem = pl.BlockSpec(memory_space=pltpu.VMEM)
    shape = jax.ShapeDtypeStruct(residual.shape, jnp.bfloat16)
    return pl.pallas_call(
        finish_kernel,
        out_shape=(shape, shape),
        in_specs=[[vmem] * len(nears), vmem, vmem, vmem, [vmem] * len(steps), vmem, vmem],
        out_specs=(vmem, vmem),
        compiler_params=pltpu.CompilerParams(vmem_limit_bytes=32 * MIB),
        name="finish",
    )(nears, far, own, came, steps, residual, norm_gain.reshape(1, -1))


def exchange(blocks, mesh_shape):
    replicas, owners = mesh_shape
    half_rep, half_dp = replicas // 2, owners // 2
    groups = []
    for side in range(2):
        for rest in range(half_rep):
            groups.append(
                [
                    (((side + owner // half_dp) % 2) * half_rep + rest) * owners + owner
                    for owner in range(owners)
                ]
            )
    return lax.all_to_all(
        blocks,
        ("rep", "dp"),
        split_axis=0,
        concat_axis=0,
        axis_index_groups=groups,
        tiled=True,
    )


def step_along(array, step, owners):
    z_size = owners // 2
    pairs = [
        (owner, owner // z_size * z_size + (owner + step) % z_size) for owner in range(owners)
    ]
    return lax.ppermute(array, "dp", pairs)


def step_across(array, mesh_shape):
    replicas, owners = mesh_shape
    pairs = [
        (
            replica * owners + owner,
            (replica + replicas // 2) % replicas * owners + (owner + owners // 2) % owners,
        )
        for replica in range(replicas)
        for owner in range(owners)
    ]
    return lax.ppermute(array, ("rep", "dp"), pairs)


def per_device(
    queries, latent_cache, new_latent, lengths, value_up, output_proj, residual, norm_gain
):
    owners = lax.axis_size("dp")
    mesh_shape = (lax.axis_size("rep"), owners)
    rows_here = latent_cache.shape[0]
    owned = value_up.shape[0]
    width = output_proj.shape[1]
    first = LEFT_COLUMNS
    latent_out, proj_near = attend(
        queries, latent_cache, new_latent, lengths, output_proj, owners
    )
    owned_latent = exchange(latent_out, mesh_shape).reshape(owners * rows_here * owned, LAT)
    values, own, send = make_values(
        owned_latent, value_up, proj_near, owners, rows_here, width - first
    )
    came = step_across(send, mesh_shape)
    parts = project(values, proj_near, owners, rows_here, first)
    nears = [parts[0]] + [step_along(parts[k], k, owners) for k in range(1, len(parts))]
    pairs = add_far(own, came)
    steps = [step_along(pair, k, owners) for k, pair in enumerate(pairs, 1)]
    far = step_across(add_near(nears), mesh_shape)
    return finish(nears, far, own, came, steps, residual, norm_gain)


def solution(mesh):
    return jax.shard_map(
        per_device,
        mesh=mesh,
        in_specs=(
            P(("rep", "dp"), None, None),
            P(("rep", "dp"), None, None),
            P(("rep", "dp"), None),
            P("rep"),
            P("dp", None, None),
            P("dp", None),
            P(("rep", "dp"), None),
            P(),
        ),
        out_specs=(P(("rep", "dp"), None), P(("rep", "dp"), None)),
        check_vma=False,
    )
```

```python
import jax
import jax.numpy as jnp
from jax import lax
from jax.experimental import pallas as pl
from jax.experimental.pallas import tpu as pltpu
from jax.sharding import PartitionSpec as P

LAT = 512
GROUP_ROWS = 4
PROJ_STEP = 1024
LEFT_COLUMNS = 3328
score_scale = 192.0 ** (-0.5)
norm_eps = 1e-06
MIB = 1024 * 1024


def attend_kernel(
    lengths_hbm, queries_hbm, latent_hbm, cache_hbm, *refs
):
    *owner_refs, out_ref = refs[:-11]
    (
        held, queries_ref, latent_ref, latent_wide, gathered_ref, softmax_ref,
        lengths_ref, order, arrived_small, arrived_first, arrived_second,
    ) = refs[-11:]
    row_count, width, span = held.shape
    owners, _, _ = out_ref.shape
    heads = queries_ref.shape[1]
    owned = heads // owners
    first_row = lax.axis_index("dp") * row_count
    pair_count = row_count // 2
    group_count = row_count // GROUP_ROWS
    group_pairs = GROUP_ROWS // 2
    short = span // 2

    lengths_copy = pltpu.make_async_copy(lengths_hbm, lengths_ref, arrived_small.at[0])
    latent_copy = pltpu.make_async_copy(latent_hbm, latent_ref, arrived_small.at[1])

    def fetch_first(group):
        rows, keys = pl.ds(group * GROUP_ROWS, GROUP_ROWS), pl.ds(0, short)
        return (
            pltpu.make_async_copy(
                queries_hbm.at[rows], queries_ref.at[rows], arrived_first.at[0, group]
            ),
            pltpu.make_async_copy(
                cache_hbm.at[rows, :, keys], held.at[rows, :, keys], arrived_first.at[1, group]
            ),
        )

    def fetch_second(slot):
        rows, keys = pl.ds(2 * order[slot], 2), pl.ds(short, short)
        return pltpu.make_async_copy(
            cache_hbm.at[rows, :, keys], held.at[rows, :, keys], arrived_second.at[slot]
        )

    def start_first(group):
        for copy in fetch_first(group):
            copy.start()

    start_first(0)
    lengths_copy.start()
    latent_copy.start()
    start_first(1)

    lengths_copy.wait()
    longest = [
        jnp.maximum(lengths_ref[first_row + 2 * pair], lengths_ref[first_row + 2 * pair + 1])
        for pair in range(pair_count)
    ]
    is_long = [(length > short).astype(jnp.int32) for length in longest]
    long_slot, short_slot = 0, sum(is_long)
    long_groups = (short_slot + group_pairs - 1) // group_pairs
    for pair in range(pair_count):
        order[jnp.where(is_long[pair] == 1, long_slot, short_slot)] = pair
        long_slot = long_slot + is_long[pair]
        short_slot = short_slot + 1 - is_long[pair]
    latent_copy.wait()
    latent_wide[...] = latent_ref[...].astype(jnp.float32)

    def score(row, start):
        scores = jnp.dot(
            queries_ref[row],
            held[row, :, start : start + short],
            preferred_element_type=jnp.float32,
        )
        position = start + lax.broadcasted_iota(jnp.int32, scores.shape, 1)
        return jnp.where(
            position < lengths_ref[first_row + row], scores * score_scale, -jnp.inf
        )

    def gather(row, start, raised):
        return lax.dot_general(
            raised.astype(jnp.bfloat16),
            held[row, :LAT, start : start + short],
            (((1,), (1,)), ((), ())),
            preferred_element_type=jnp.float32,
        )

    def weigh_first(row, scores):
        fresh = latent_wide[pl.ds(row, 1), :]
        self_score = (
            jnp.sum(queries_ref[row].astype(jnp.float32) * fresh, axis=1, keepdims=True)
            * score_scale
        )
        row_max = jnp.maximum(jnp.max(scores, axis=1, keepdims=True), self_score)
        raised = jnp.exp(scores - row_max)
        self_raised = jnp.exp(self_score - row_max)
        row_total = jnp.sum(raised, axis=1, keepdims=True) + self_raised
        self_weight = self_raised.astype(jnp.bfloat16).astype(jnp.float32)
        softmax_ref[row, :, 0:1] = row_max
        softmax_ref[row, :, 1:2] = row_total
        return raised, self_weight * fresh[:, :LAT], row_total

    def weigh_second(row, scores):
        old_max = softmax_ref[row, :, 0:1]
        row_max = jnp.maximum(jnp.max(scores, axis=1, keepdims=True), old_max)
        raised = jnp.exp(scores - row_max)
        kept = jnp.exp(old_max - row_max)
        row_total = softmax_ref[row, :, 1:2] * kept + jnp.sum(raised, axis=1, keepdims=True)
        return raised, kept, row_total

    def first_half(group, carry):
        for copy in fetch_first(group):
            copy.wait()

        @pl.when(group + 2 < group_count)
        def _():
            start_first(group + 2)

        @pl.when(group == group_count - 2)
        def _():
            def start(slot, carry):
                fetch_second(slot).start()
                return carry

            lax.fori_loop(0, long_groups * group_pairs, start, 0)

        rows = [group * GROUP_ROWS + i for i in range(GROUP_ROWS)]
        scores = [score(row, 0) for row in rows]
        weighed = [weigh_first(row, some) for row, some in zip(rows, scores)]
        done = []
        for row, (raised, fresh_part, row_total) in zip(rows, weighed):
            gathered = gather(row, 0, raised) + fresh_part
            gathered_ref[row] = gathered
            done.append((gathered / row_total).reshape(owners, owned, LAT))
        size = GROUP_ROWS * owned
        out_ref[:, pl.ds(pl.multiple_of(group * size, size), size), :] = jnp.concatenate(
            done, axis=1
        ).astype(jnp.bfloat16)
        return carry

    def second_half(group, carry):
        slots = [group * group_pairs + i for i in range(group_pairs)]
        for slot in slots:
            fetch_second(slot).wait()
        pairs = [order[slot] for slot in slots]
        rows = [2 * pair + i for pair in pairs for i in range(2)]
        scores = [score(row, short) for row in rows]
        weighed = [weigh_second(row, some) for row, some in zip(rows, scores)]
        done = []
        for row, (raised, kept, row_total) in zip(rows, weighed):
            gathered = gather(row, short, raised) + gathered_ref[row] * kept
            done.append((gathered / row_total).reshape(owners, owned, LAT))
        size = 2 * owned
        for i, pair in enumerate(pairs):
            out_ref[:, pl.ds(pl.multiple_of(pair * size, size), size), :] = jnp.concatenate(
                done[2 * i : 2 * i + 2], axis=1
            ).astype(jnp.bfloat16)
        return carry

    lax.fori_loop(0, group_count, first_half, 0)
    lax.fori_loop(0, long_groups, second_half, 0)
    here = lax.axis_index("dp")
    z_size = owners // 2
    for place, owner_ref in enumerate(owner_refs):
        far = (here // z_size + place // z_size) % 2
        owner_ref[...] = out_ref[far * z_size + (here + place) % z_size]


def attend(queries, latent_cache, new_latent, lengths, owners):
    row_count, span, width = latent_cache.shape
    heads = queries.shape[1]
    owned = heads // owners
    vmem = pl.BlockSpec(memory_space=pltpu.VMEM)
    hbm = pl.BlockSpec(memory_space=pltpu.HBM)
    arrays = (lengths, queries, new_latent, jnp.swapaxes(latent_cache, 1, 2))
    return pl.pallas_call(
        attend_kernel,
        out_shape=[jax.ShapeDtypeStruct((row_count * owned, LAT), jnp.bfloat16)] * owners,
        in_specs=[hbm] * len(arrays),
        out_specs=[vmem] * owners,
        scratch_shapes=[
            pltpu.VMEM((owners, row_count * owned, LAT), jnp.bfloat16),
            pltpu.VMEM((row_count, width, span), jnp.bfloat16),
            pltpu.VMEM(queries.shape, jnp.bfloat16),
            pltpu.VMEM(new_latent.shape, jnp.bfloat16),
            pltpu.VMEM(new_latent.shape, jnp.float32),
            pltpu.VMEM((row_count, heads, LAT), jnp.float32),
            pltpu.VMEM((row_count, heads, 128), jnp.float32),
            pltpu.SMEM(lengths.shape, jnp.int32),
            pltpu.SMEM((row_count // 2,), jnp.int32),
            pltpu.SemaphoreType.DMA((2,)),
            pltpu.SemaphoreType.DMA((2, row_count // GROUP_ROWS)),
            pltpu.SemaphoreType.DMA((row_count // 2,)),
        ],
        cost_estimate=pl.CostEstimate(
            flops=4 * row_count * heads * span * width,
            bytes_accessed=2 * row_count * span * width,
            transcendentals=row_count * heads * span,
        ),
        compiler_params=pltpu.CompilerParams(vmem_limit_bytes=24 * MIB),
        name="attend",
    )(*(pltpu.with_memory_space_constraint(x, pltpu.HBM) for x in arrays))


def bring_kernel(after_hbm, proj_hbm, proj_ref, arrived):
    del after_hbm
    copy = pltpu.make_async_copy(proj_hbm, proj_ref, arrived)
    copy.start()
    copy.wait()


def bring(output_proj, after):
    return pl.pallas_call(
        bring_kernel,
        out_shape=pltpu.VMEM(output_proj.shape, jnp.bfloat16),
        in_specs=[pl.BlockSpec(memory_space=pl.ANY), pl.BlockSpec(memory_space=pltpu.HBM)],
        out_specs=pl.BlockSpec(memory_space=pltpu.VMEM),
        scratch_shapes=[pltpu.SemaphoreType.DMA],
        cost_estimate=pl.CostEstimate(
            flops=0, bytes_accessed=2 * output_proj.size, transcendentals=0
        ),
        compiler_params=pltpu.CompilerParams(vmem_limit_bytes=16 * MIB),
        name="bring",
    )(after, pltpu.with_memory_space_constraint(output_proj, pltpu.HBM))


def values_kernel(latent_refs, value_up_ref, proj_ref, values_ref, own_ref, send_ref, wide):
    owned, lat, value_size = value_up_ref.shape
    owners, rows_here, columns = 2 * own_ref.shape[0], own_ref.shape[1], own_ref.shape[2]
    rows = owners * rows_here
    z_size = owners // 2

    size = rows_here * owned
    for place, latent_ref in enumerate(latent_refs):
        far, step = place // z_size, place % z_size
        back = (far * z_size + (z_size - step) % z_size) * size
        for c in range(lat // 128):
            wide[c, back : back + size] = latent_ref[:, c * 128 : (c + 1) * 128].astype(
                jnp.float32
            )
    for h in range(owned):
        mine = jnp.concatenate(
            [wide[c, pl.ds(h, rows, stride=owned), :] for c in range(lat // 128)], axis=1
        ).astype(jnp.bfloat16)
        values_ref[:, h * value_size : (h + 1) * value_size] = jnp.dot(
            mine, value_up_ref[h], preferred_element_type=jnp.float32
        ).astype(jnp.bfloat16)
    flattened = values_ref[...]
    for start in range(0, columns, PROJ_STEP):
        stop = min(start + PROJ_STEP, columns)
        done = jnp.dot(
            flattened,
            proj_ref[:, LEFT_COLUMNS + start : LEFT_COLUMNS + stop],
            preferred_element_type=jnp.float32,
        ).astype(jnp.bfloat16)
        done = done.reshape(2, z_size, rows_here, stop - start)
        own_ref[:, :, start:stop] = done[0]
        send_ref[:, :, start:stop] = done[1]


def make_values(owned_latents, value_up, output_proj, owners, rows_here):
    owned, lat, value_size = value_up.shape
    depth, width = output_proj.shape
    columns = width - LEFT_COLUMNS
    rows = owners * rows_here
    vmem = pl.BlockSpec(memory_space=pltpu.VMEM)
    half = jax.ShapeDtypeStruct((owners // 2, rows_here, columns), jnp.bfloat16)
    return pl.pallas_call(
        values_kernel,
        out_shape=(jax.ShapeDtypeStruct((rows, owned * value_size), jnp.bfloat16), half, half),
        in_specs=[[vmem] * owners, vmem, vmem],
        out_specs=(vmem, vmem, vmem),
        scratch_shapes=[pltpu.VMEM((lat // 128, rows * owned, 128), jnp.float32)],
        cost_estimate=pl.CostEstimate(
            flops=2 * rows * depth * columns, bytes_accessed=2 * depth * columns, transcendentals=0
        ),
        compiler_params=pltpu.CompilerParams(vmem_limit_bytes=20 * MIB),
        name="values",
    )(owned_latents, value_up, pltpu.with_memory_space_constraint(output_proj, pltpu.VMEM))


def project_kernel(values_ref, proj_ref, *out_refs):
    rows_here, columns = out_refs[0].shape[1:]
    z_size = len(out_refs)
    flattened = values_ref[...]
    for start in range(0, columns, PROJ_STEP):
        stop = min(start + PROJ_STEP, columns)
        done = jnp.dot(
            flattened, proj_ref[:, start:stop], preferred_element_type=jnp.float32
        ).astype(jnp.bfloat16)
        done = done.reshape(2, z_size, rows_here, stop - start)
        for step in range(z_size):
            out_refs[step][:, :, start:stop] = done[:, step]


def project(values, output_proj, owners, rows_here):
    rows, depth = values.shape
    columns = LEFT_COLUMNS
    z_size = owners // 2
    vmem = pl.BlockSpec(memory_space=pltpu.VMEM)
    part = jax.ShapeDtypeStruct((2, rows_here, columns), jnp.bfloat16)
    return pl.pallas_call(
        project_kernel,
        out_shape=[part] * z_size,
        in_specs=[vmem, vmem],
        out_specs=[vmem] * z_size,
        cost_estimate=pl.CostEstimate(
            flops=2 * rows * depth * columns, bytes_accessed=2 * depth * columns, transcendentals=0
        ),
        compiler_params=pltpu.CompilerParams(vmem_limit_bytes=20 * MIB),
        name="project",
    )(values, pltpu.with_memory_space_constraint(output_proj, pltpu.VMEM))


def add_far_kernel(own_ref, came_ref, *out_refs):
    for step, out_ref in enumerate(out_refs, 1):
        both = own_ref[step].astype(jnp.float32) + came_ref[step].astype(jnp.float32)
        out_ref[...] = both.astype(jnp.bfloat16)


def add_far(own, came):
    vmem = pl.BlockSpec(memory_space=pltpu.VMEM)
    return pl.pallas_call(
        add_far_kernel,
        out_shape=[jax.ShapeDtypeStruct(own.shape[1:], jnp.bfloat16)] * (own.shape[0] - 1),
        in_specs=[vmem, vmem],
        out_specs=[vmem] * (own.shape[0] - 1),
        cost_estimate=pl.CostEstimate(flops=own.size, bytes_accessed=own.size * 6, transcendentals=0),
        compiler_params=pltpu.CompilerParams(vmem_limit_bytes=16 * MIB),
        name="add_far",
    )(own, came)


def add_near_kernel(*refs):
    *part_refs, out_ref = refs
    total = part_refs[0][1].astype(jnp.float32)
    for part_ref in part_refs[1:]:
        total = total + part_ref[1].astype(jnp.float32)
    out_ref[...] = total.astype(jnp.bfloat16)


def add_near(parts):
    vmem = pl.BlockSpec(memory_space=pltpu.VMEM)
    return pl.pallas_call(
        add_near_kernel,
        out_shape=jax.ShapeDtypeStruct(parts[0].shape[1:], jnp.bfloat16),
        in_specs=[vmem] * len(parts),
        out_specs=vmem,
        cost_estimate=pl.CostEstimate(
            flops=parts[0].size * 2, bytes_accessed=parts[0].size * 8, transcendentals=0
        ),
        compiler_params=pltpu.CompilerParams(vmem_limit_bytes=16 * MIB),
        name="add_near",
    )(*parts)


def finish_kernel(near_refs, far_ref, own_ref, came_ref, step_refs, residual_ref, gain_ref,
                  hidden_ref, normed_ref):
    rows, first = far_ref.shape
    width = residual_ref.shape[1]
    left = residual_ref[:, :first].astype(jnp.float32) + far_ref[...].astype(jnp.float32)
    for near_ref in near_refs:
        left = left + near_ref[0].astype(jnp.float32)
    right = residual_ref[:, first:].astype(jnp.float32) + (
        own_ref[0].astype(jnp.float32) + came_ref[0].astype(jnp.float32)
    )
    for step_ref in step_refs:
        right = right + step_ref[...].astype(jnp.float32)
    total = jnp.sum(left * left, axis=1, keepdims=True) + jnp.sum(
        right * right, axis=1, keepdims=True
    )
    inverse_rms = lax.rsqrt(total * (1.0 / width) + norm_eps)
    for part, here in ((left, slice(0, first)), (right, slice(first, width))):
        hidden_ref[:, here] = part.astype(jnp.bfloat16)
        normed = part * inverse_rms * gain_ref[:, here].astype(jnp.float32)
        normed_ref[:, here] = normed.astype(jnp.bfloat16)


def finish(nears, far, own, came, steps, residual, norm_gain):
    vmem = pl.BlockSpec(memory_space=pltpu.VMEM)
    shape = jax.ShapeDtypeStruct(residual.shape, jnp.bfloat16)
    return pl.pallas_call(
        finish_kernel,
        out_shape=(shape, shape),
        in_specs=[[vmem] * len(nears), vmem, vmem, vmem, [vmem] * len(steps), vmem, vmem],
        out_specs=(vmem, vmem),
        compiler_params=pltpu.CompilerParams(vmem_limit_bytes=32 * MIB),
        name="finish",
    )(nears, far, own, came, steps, residual, norm_gain.reshape(1, -1))


def send(array, far, step, mesh_shape):
    replicas, owners = mesh_shape
    z_size = owners // 2
    pairs = []
    for replica in range(replicas):
        for owner in range(owners):
            to_replica = (replica + far * (replicas // 2)) % replicas
            to_half = (owner // z_size + far) % 2
            to_owner = to_half * z_size + (owner + step) % z_size
            pairs.append((replica * owners + owner, to_replica * owners + to_owner))
    return lax.ppermute(array, ("rep", "dp"), pairs)


def per_device(
    queries, latent_cache, new_latent, lengths, value_up, output_proj, residual, norm_gain
):
    owners = lax.axis_size("dp")
    mesh_shape = (lax.axis_size("rep"), owners)
    rows_here = latent_cache.shape[0]
    z_size = owners // 2
    latents = attend(queries, latent_cache, new_latent, lengths, owners)
    owned_latents = [latents[0]] + [
        send(latents[place], place // z_size, place % z_size, mesh_shape)
        for place in range(1, owners)
    ]
    proj_near = bring(output_proj, latents[0])
    values, own, across = make_values(owned_latents, value_up, proj_near, owners, rows_here)
    came = send(across, 1, 0, mesh_shape)
    parts = project(values, proj_near, owners, rows_here)
    nears = [parts[0]] + [send(parts[k], 0, k, mesh_shape) for k in range(1, z_size)]
    pairs = add_far(own, came)
    steps = [send(pair, 0, k, mesh_shape) for k, pair in enumerate(pairs, 1)]
    far = send(add_near(nears), 1, 0, mesh_shape)
    return finish(nears, far, own, came, steps, residual, norm_gain)


def solution(mesh):
    return jax.shard_map(
        per_device,
        mesh=mesh,
        in_specs=(
            P(("rep", "dp"), None, None),
            P(("rep", "dp"), None, None),
            P(("rep", "dp"), None),
            P("rep"),
            P("dp", None, None),
            P("dp", None),
            P(("rep", "dp"), None),
            P(),
        ),
        out_specs=(P(("rep", "dp"), None), P(("rep", "dp"), None)),
        check_vma=False,
    )
```

```python
import jax
import jax.numpy as jnp
from jax import lax
from jax.experimental import pallas as pl
from jax.experimental.pallas import tpu as pltpu
from jax.sharding import PartitionSpec as P

LAT = 512
GROUP_ROWS = 4
PROJ_STEP = 1024
LEFT_COLUMNS = 3328
ORDER = (6, 5, 7, 4, 2, 1, 3)
score_scale = 192.0 ** (-0.5)
norm_eps = 1e-06
MIB = 1024 * 1024


def attend_kernel(
    lengths_hbm, queries_hbm, latent_hbm, cache_hbm, *refs
):
    *owner_refs, out_ref = refs[:-11]
    (
        held, queries_ref, latent_ref, latent_wide, gathered_ref, softmax_ref,
        lengths_ref, order, arrived_small, arrived_first, arrived_second,
    ) = refs[-11:]
    row_count, width, span = held.shape
    owners, _, _ = out_ref.shape
    heads = queries_ref.shape[1]
    owned = heads // owners
    first_row = lax.axis_index("dp") * row_count
    pair_count = row_count // 2
    group_count = row_count // GROUP_ROWS
    group_pairs = GROUP_ROWS // 2
    short = span // 2

    lengths_copy = pltpu.make_async_copy(lengths_hbm, lengths_ref, arrived_small.at[0])
    latent_copy = pltpu.make_async_copy(latent_hbm, latent_ref, arrived_small.at[1])

    def fetch_first(group):
        rows, keys = pl.ds(group * GROUP_ROWS, GROUP_ROWS), pl.ds(0, short)
        return (
            pltpu.make_async_copy(
                queries_hbm.at[rows], queries_ref.at[rows], arrived_first.at[0, group]
            ),
            pltpu.make_async_copy(
                cache_hbm.at[rows, :, keys], held.at[rows, :, keys], arrived_first.at[1, group]
            ),
        )

    def fetch_second(slot):
        rows, keys = pl.ds(2 * order[slot], 2), pl.ds(short, short)
        return pltpu.make_async_copy(
            cache_hbm.at[rows, :, keys], held.at[rows, :, keys], arrived_second.at[slot]
        )

    def start_first(group):
        for copy in fetch_first(group):
            copy.start()

    start_first(0)
    lengths_copy.start()
    latent_copy.start()
    start_first(1)

    lengths_copy.wait()
    longest = [
        jnp.maximum(lengths_ref[first_row + 2 * pair], lengths_ref[first_row + 2 * pair + 1])
        for pair in range(pair_count)
    ]
    is_long = [(length > short).astype(jnp.int32) for length in longest]
    long_slot, short_slot = 0, sum(is_long)
    long_groups = (short_slot + group_pairs - 1) // group_pairs
    for pair in range(pair_count):
        order[jnp.where(is_long[pair] == 1, long_slot, short_slot)] = pair
        long_slot = long_slot + is_long[pair]
        short_slot = short_slot + 1 - is_long[pair]
    latent_copy.wait()
    latent_wide[...] = latent_ref[...].astype(jnp.float32)

    def score(row, start):
        scores = jnp.dot(
            queries_ref[row],
            held[row, :, start : start + short],
            preferred_element_type=jnp.float32,
        )
        position = start + lax.broadcasted_iota(jnp.int32, scores.shape, 1)
        return jnp.where(
            position < lengths_ref[first_row + row], scores * score_scale, -jnp.inf
        )

    def gather(row, start, raised):
        return lax.dot_general(
            raised.astype(jnp.bfloat16),
            held[row, :LAT, start : start + short],
            (((1,), (1,)), ((), ())),
            preferred_element_type=jnp.float32,
        )

    def weigh_first(row, scores):
        fresh = latent_wide[pl.ds(row, 1), :]
        self_score = (
            jnp.sum(queries_ref[row].astype(jnp.float32) * fresh, axis=1, keepdims=True)
            * score_scale
        )
        row_max = jnp.maximum(jnp.max(scores, axis=1, keepdims=True), self_score)
        raised = jnp.exp(scores - row_max)
        self_raised = jnp.exp(self_score - row_max)
        row_total = jnp.sum(raised, axis=1, keepdims=True) + self_raised
        self_weight = self_raised.astype(jnp.bfloat16).astype(jnp.float32)
        softmax_ref[row, :, 0:1] = row_max
        softmax_ref[row, :, 1:2] = row_total
        return raised, self_weight * fresh[:, :LAT], row_total

    def weigh_second(row, scores):
        old_max = softmax_ref[row, :, 0:1]
        row_max = jnp.maximum(jnp.max(scores, axis=1, keepdims=True), old_max)
        raised = jnp.exp(scores - row_max)
        kept = jnp.exp(old_max - row_max)
        row_total = softmax_ref[row, :, 1:2] * kept + jnp.sum(raised, axis=1, keepdims=True)
        return raised, kept, row_total

    def first_half(group, carry):
        for copy in fetch_first(group):
            copy.wait()

        @pl.when(group + 2 < group_count)
        def _():
            start_first(group + 2)

        @pl.when(group == group_count - 2)
        def _():
            def start(slot, carry):
                fetch_second(slot).start()
                return carry

            lax.fori_loop(0, long_groups * group_pairs, start, 0)

        rows = [group * GROUP_ROWS + i for i in range(GROUP_ROWS)]
        scores = [score(row, 0) for row in rows]
        weighed = [weigh_first(row, some) for row, some in zip(rows, scores)]
        done = []
        for row, (raised, fresh_part, row_total) in zip(rows, weighed):
            gathered = gather(row, 0, raised) + fresh_part
            gathered_ref[row] = gathered
            done.append((gathered / row_total).reshape(owners, owned, LAT))
        size = GROUP_ROWS * owned
        out_ref[:, pl.ds(pl.multiple_of(group * size, size), size), :] = jnp.concatenate(
            done, axis=1
        ).astype(jnp.bfloat16)
        return carry

    def second_half(group, carry):
        slots = [group * group_pairs + i for i in range(group_pairs)]
        for slot in slots:
            fetch_second(slot).wait()
        pairs = [order[slot] for slot in slots]
        rows = [2 * pair + i for pair in pairs for i in range(2)]
        scores = [score(row, short) for row in rows]
        weighed = [weigh_second(row, some) for row, some in zip(rows, scores)]
        done = []
        for row, (raised, kept, row_total) in zip(rows, weighed):
            gathered = gather(row, short, raised) + gathered_ref[row] * kept
            done.append((gathered / row_total).reshape(owners, owned, LAT))
        size = 2 * owned
        for i, pair in enumerate(pairs):
            out_ref[:, pl.ds(pl.multiple_of(pair * size, size), size), :] = jnp.concatenate(
                done[2 * i : 2 * i + 2], axis=1
            ).astype(jnp.bfloat16)
        return carry

    lax.fori_loop(0, group_count, first_half, 0)
    lax.fori_loop(0, long_groups, second_half, 0)
    here = lax.axis_index("dp")
    z_size = owners // 2
    for place, owner_ref in enumerate(owner_refs):
        far = (here // z_size + place // z_size) % 2
        owner_ref[...] = out_ref[far * z_size + (here + place) % z_size]


def attend(queries, latent_cache, new_latent, lengths, owners):
    row_count, span, width = latent_cache.shape
    heads = queries.shape[1]
    owned = heads // owners
    vmem = pl.BlockSpec(memory_space=pltpu.VMEM)
    hbm = pl.BlockSpec(memory_space=pltpu.HBM)
    arrays = (lengths, queries, new_latent, jnp.swapaxes(latent_cache, 1, 2))
    return pl.pallas_call(
        attend_kernel,
        out_shape=[jax.ShapeDtypeStruct((row_count * owned, LAT), jnp.bfloat16)] * owners,
        in_specs=[hbm] * len(arrays),
        out_specs=[vmem] * owners,
        scratch_shapes=[
            pltpu.VMEM((owners, row_count * owned, LAT), jnp.bfloat16),
            pltpu.VMEM((row_count, width, span), jnp.bfloat16),
            pltpu.VMEM(queries.shape, jnp.bfloat16),
            pltpu.VMEM(new_latent.shape, jnp.bfloat16),
            pltpu.VMEM(new_latent.shape, jnp.float32),
            pltpu.VMEM((row_count, heads, LAT), jnp.float32),
            pltpu.VMEM((row_count, heads, 128), jnp.float32),
            pltpu.SMEM(lengths.shape, jnp.int32),
            pltpu.SMEM((row_count // 2,), jnp.int32),
            pltpu.SemaphoreType.DMA((2,)),
            pltpu.SemaphoreType.DMA((2, row_count // GROUP_ROWS)),
            pltpu.SemaphoreType.DMA((row_count // 2,)),
        ],
        cost_estimate=pl.CostEstimate(
            flops=4 * row_count * heads * span * width,
            bytes_accessed=2 * row_count * span * width,
            transcendentals=row_count * heads * span,
        ),
        compiler_params=pltpu.CompilerParams(vmem_limit_bytes=24 * MIB),
        name="attend",
    )(*(pltpu.with_memory_space_constraint(x, pltpu.HBM) for x in arrays))


def bring_kernel(after_hbm, proj_hbm, proj_ref, arrived):
    del after_hbm
    copy = pltpu.make_async_copy(proj_hbm, proj_ref, arrived)
    copy.start()
    copy.wait()


def bring(output_proj, after):
    return pl.pallas_call(
        bring_kernel,
        out_shape=pltpu.VMEM(output_proj.shape, jnp.bfloat16),
        in_specs=[pl.BlockSpec(memory_space=pl.ANY), pl.BlockSpec(memory_space=pltpu.HBM)],
        out_specs=pl.BlockSpec(memory_space=pltpu.VMEM),
        scratch_shapes=[pltpu.SemaphoreType.DMA],
        cost_estimate=pl.CostEstimate(
            flops=0, bytes_accessed=2 * output_proj.size, transcendentals=0
        ),
        compiler_params=pltpu.CompilerParams(vmem_limit_bytes=16 * MIB),
        name="bring",
    )(after, pltpu.with_memory_space_constraint(output_proj, pltpu.HBM))


def values_kernel(latent_refs, value_up_ref, proj_ref, values_ref, own_ref, send_ref, wide):
    owned, lat, value_size = value_up_ref.shape
    owners, rows_here, columns = 2 * own_ref.shape[0], own_ref.shape[1], own_ref.shape[2]
    rows = owners * rows_here
    z_size = owners // 2

    size = rows_here * owned
    for place, latent_ref in zip((0,) + ORDER, latent_refs):
        far, step = place // z_size, place % z_size
        back = (far * z_size + (z_size - step) % z_size) * size
        for c in range(lat // 128):
            wide[c, back : back + size] = latent_ref[:, c * 128 : (c + 1) * 128].astype(
                jnp.float32
            )
    for h in range(owned):
        mine = jnp.concatenate(
            [wide[c, pl.ds(h, rows, stride=owned), :] for c in range(lat // 128)], axis=1
        ).astype(jnp.bfloat16)
        values_ref[:, h * value_size : (h + 1) * value_size] = jnp.dot(
            mine, value_up_ref[h], preferred_element_type=jnp.float32
        ).astype(jnp.bfloat16)
    flattened = values_ref[...]
    for start in range(0, columns, PROJ_STEP):
        stop = min(start + PROJ_STEP, columns)
        done = jnp.dot(
            flattened,
            proj_ref[:, LEFT_COLUMNS + start : LEFT_COLUMNS + stop],
            preferred_element_type=jnp.float32,
        ).astype(jnp.bfloat16)
        done = done.reshape(2, z_size, rows_here, stop - start)
        own_ref[:, :, start:stop] = done[0]
        send_ref[:, :, start:stop] = done[1]


def make_values(owned_latents, value_up, output_proj, owners, rows_here):
    owned, lat, value_size = value_up.shape
    depth, width = output_proj.shape
    columns = width - LEFT_COLUMNS
    rows = owners * rows_here
    vmem = pl.BlockSpec(memory_space=pltpu.VMEM)
    half = jax.ShapeDtypeStruct((owners // 2, rows_here, columns), jnp.bfloat16)
    return pl.pallas_call(
        values_kernel,
        out_shape=(jax.ShapeDtypeStruct((rows, owned * value_size), jnp.bfloat16), half, half),
        in_specs=[[vmem] * owners, vmem, vmem],
        out_specs=(vmem, vmem, vmem),
        scratch_shapes=[pltpu.VMEM((lat // 128, rows * owned, 128), jnp.float32)],
        cost_estimate=pl.CostEstimate(
            flops=2 * rows * depth * columns, bytes_accessed=2 * depth * columns, transcendentals=0
        ),
        compiler_params=pltpu.CompilerParams(vmem_limit_bytes=20 * MIB),
        name="values",
    )(owned_latents, value_up, pltpu.with_memory_space_constraint(output_proj, pltpu.VMEM))


def project_kernel(values_ref, proj_ref, *out_refs):
    rows_here, columns = out_refs[0].shape[1:]
    z_size = len(out_refs)
    flattened = values_ref[...]
    for start in range(0, columns, PROJ_STEP):
        stop = min(start + PROJ_STEP, columns)
        done = jnp.dot(
            flattened, proj_ref[:, start:stop], preferred_element_type=jnp.float32
        ).astype(jnp.bfloat16)
        done = done.reshape(2, z_size, rows_here, stop - start)
        for step in range(z_size):
            out_refs[step][:, :, start:stop] = done[:, step]


def project(values, output_proj, owners, rows_here):
    rows, depth = values.shape
    columns = LEFT_COLUMNS
    z_size = owners // 2
    vmem = pl.BlockSpec(memory_space=pltpu.VMEM)
    part = jax.ShapeDtypeStruct((2, rows_here, columns), jnp.bfloat16)
    return pl.pallas_call(
        project_kernel,
        out_shape=[part] * z_size,
        in_specs=[vmem, vmem],
        out_specs=[vmem] * z_size,
        cost_estimate=pl.CostEstimate(
            flops=2 * rows * depth * columns, bytes_accessed=2 * depth * columns, transcendentals=0
        ),
        compiler_params=pltpu.CompilerParams(vmem_limit_bytes=20 * MIB),
        name="project",
    )(values, pltpu.with_memory_space_constraint(output_proj, pltpu.VMEM))


def add_far_kernel(own_ref, came_ref, *out_refs):
    for step, out_ref in enumerate(out_refs, 1):
        both = own_ref[step].astype(jnp.float32) + came_ref[step].astype(jnp.float32)
        out_ref[...] = both.astype(jnp.bfloat16)


def add_far(own, came):
    vmem = pl.BlockSpec(memory_space=pltpu.VMEM)
    return pl.pallas_call(
        add_far_kernel,
        out_shape=[jax.ShapeDtypeStruct(own.shape[1:], jnp.bfloat16)] * (own.shape[0] - 1),
        in_specs=[vmem, vmem],
        out_specs=[vmem] * (own.shape[0] - 1),
        cost_estimate=pl.CostEstimate(flops=own.size, bytes_accessed=own.size * 6, transcendentals=0),
        compiler_params=pltpu.CompilerParams(vmem_limit_bytes=16 * MIB),
        name="add_far",
    )(own, came)


def add_near_kernel(*refs):
    *part_refs, out_ref = refs
    total = part_refs[0][1].astype(jnp.float32)
    for part_ref in part_refs[1:]:
        total = total + part_ref[1].astype(jnp.float32)
    out_ref[...] = total.astype(jnp.bfloat16)


def add_near(parts):
    vmem = pl.BlockSpec(memory_space=pltpu.VMEM)
    return pl.pallas_call(
        add_near_kernel,
        out_shape=jax.ShapeDtypeStruct(parts[0].shape[1:], jnp.bfloat16),
        in_specs=[vmem] * len(parts),
        out_specs=vmem,
        cost_estimate=pl.CostEstimate(
            flops=parts[0].size * 2, bytes_accessed=parts[0].size * 8, transcendentals=0
        ),
        compiler_params=pltpu.CompilerParams(vmem_limit_bytes=16 * MIB),
        name="add_near",
    )(*parts)


def finish_kernel(near_refs, far_ref, own_ref, came_ref, step_refs, residual_ref, gain_ref,
                  hidden_ref, normed_ref):
    rows, first = far_ref.shape
    width = residual_ref.shape[1]
    left = residual_ref[:, :first].astype(jnp.float32) + far_ref[...].astype(jnp.float32)
    for near_ref in near_refs:
        left = left + near_ref[0].astype(jnp.float32)
    right = residual_ref[:, first:].astype(jnp.float32) + (
        own_ref[0].astype(jnp.float32) + came_ref[0].astype(jnp.float32)
    )
    for step_ref in step_refs:
        right = right + step_ref[...].astype(jnp.float32)
    total = jnp.sum(left * left, axis=1, keepdims=True) + jnp.sum(
        right * right, axis=1, keepdims=True
    )
    inverse_rms = lax.rsqrt(total * (1.0 / width) + norm_eps)
    for part, here in ((left, slice(0, first)), (right, slice(first, width))):
        hidden_ref[:, here] = part.astype(jnp.bfloat16)
        normed = part * inverse_rms * gain_ref[:, here].astype(jnp.float32)
        normed_ref[:, here] = normed.astype(jnp.bfloat16)


def finish(nears, far, own, came, steps, residual, norm_gain):
    vmem = pl.BlockSpec(memory_space=pltpu.VMEM)
    shape = jax.ShapeDtypeStruct(residual.shape, jnp.bfloat16)
    return pl.pallas_call(
        finish_kernel,
        out_shape=(shape, shape),
        in_specs=[[vmem] * len(nears), vmem, vmem, vmem, [vmem] * len(steps), vmem, vmem],
        out_specs=(vmem, vmem),
        compiler_params=pltpu.CompilerParams(vmem_limit_bytes=32 * MIB),
        name="finish",
    )(nears, far, own, came, steps, residual, norm_gain.reshape(1, -1))


def send(array, far, step, mesh_shape):
    replicas, owners = mesh_shape
    z_size = owners // 2
    pairs = []
    for replica in range(replicas):
        for owner in range(owners):
            to_replica = (replica + far * (replicas // 2)) % replicas
            to_half = (owner // z_size + far) % 2
            to_owner = to_half * z_size + (owner + step) % z_size
            pairs.append((replica * owners + owner, to_replica * owners + to_owner))
    return lax.ppermute(array, ("rep", "dp"), pairs)


def per_device(
    queries, latent_cache, new_latent, lengths, value_up, output_proj, residual, norm_gain
):
    owners = lax.axis_size("dp")
    mesh_shape = (lax.axis_size("rep"), owners)
    rows_here = latent_cache.shape[0]
    z_size = owners // 2
    latents = attend(queries, latent_cache, new_latent, lengths, owners)
    owned_latents = [latents[0]] + [
        send(latents[place], place // z_size, place % z_size, mesh_shape)
        for place in ORDER
    ]
    proj_near = bring(output_proj, latents[0])
    values, own, across = make_values(owned_latents, value_up, proj_near, owners, rows_here)
    came = send(across, 1, 0, mesh_shape)
    parts = project(values, proj_near, owners, rows_here)
    nears = [parts[0]] + [send(parts[k], 0, k, mesh_shape) for k in range(1, z_size)]
    pairs = add_far(own, came)
    steps = [send(pair, 0, k, mesh_shape) for k, pair in enumerate(pairs, 1)]
    far = send(add_near(nears), 1, 0, mesh_shape)
    return finish(nears, far, own, came, steps, residual, norm_gain)


def solution(mesh):
    return jax.shard_map(
        per_device,
        mesh=mesh,
        in_specs=(
            P(("rep", "dp"), None, None),
            P(("rep", "dp"), None, None),
            P(("rep", "dp"), None),
            P("rep"),
            P("dp", None, None),
            P("dp", None),
            P(("rep", "dp"), None),
            P(),
        ),
        out_specs=(P(("rep", "dp"), None), P(("rep", "dp"), None)),
        check_vma=False,
    )
```

```python
import jax
import jax.numpy as jnp
from jax import lax
from jax.experimental import pallas as pl
from jax.experimental.pallas import tpu as pltpu
from jax.sharding import PartitionSpec as P

LAT = 512
GROUP_ROWS = 4
PROJ_STEP = 1024
LEFT_COLUMNS = 3456
ORDER = (6, 5, 7, 4, 2, 1, 3)
exponent_scale = 192.0 ** (-0.5) * 1.4426950408889634
norm_eps = 1e-06
MIB = 1024 * 1024


def attend_kernel(
    lengths_hbm, queries_hbm, latent_hbm, cache_hbm, *refs
):
    *owner_refs, out_ref = refs[:-9]
    (
        held, queries_ref, latent_ref, latent_wide,
        lengths_ref, order, arrived_small, arrived_queries, arrived_keys,
    ) = refs[-9:]
    row_count, width, span = held.shape
    owners, _, _ = out_ref.shape
    heads = queries_ref.shape[1]
    owned = heads // owners
    first_row = lax.axis_index("dp") * row_count
    pair_count = row_count // 2
    group_pairs = GROUP_ROWS // 2
    group_count = pair_count // group_pairs
    short = span // 2

    lengths_copy = pltpu.make_async_copy(lengths_hbm, lengths_ref, arrived_small.at[0])
    latent_copy = pltpu.make_async_copy(latent_hbm, latent_ref, arrived_small.at[1])

    def fetch_queries(pair):
        rows = pl.ds(2 * pair, 2)
        return pltpu.make_async_copy(
            queries_hbm.at[rows], queries_ref.at[rows], arrived_queries.at[pair]
        )

    def fetch_keys(pair, keys):
        rows = pl.ds(2 * pair, 2)
        return pltpu.make_async_copy(
            cache_hbm.at[rows, :, pl.ds(0, keys)],
            held.at[rows, :, pl.ds(0, keys)],
            arrived_keys.at[pair],
        )

    for pair in range(group_pairs):
        order[pair] = pair
        fetch_queries(pair).start()
        fetch_keys(pair, span).start()
    lengths_copy.start()
    latent_copy.start()
    lengths_copy.wait()
    longest = [
        jnp.maximum(lengths_ref[first_row + 2 * pair], lengths_ref[first_row + 2 * pair + 1])
        for pair in range(pair_count)
    ]
    is_long = [(length > short).astype(jnp.int32) for length in longest]

    short_slot = group_pairs
    long_slot = pair_count - sum(is_long[group_pairs:])
    first_is_long = sum(is_long[:group_pairs]) > 0
    short_groups = long_slot // group_pairs
    for pair in range(group_pairs, pair_count):
        order[jnp.where(is_long[pair] == 1, long_slot, short_slot)] = pair
        long_slot = long_slot + is_long[pair]
        short_slot = short_slot + 1 - is_long[pair]

    def start(group):
        for pair in [order[group * group_pairs + i] for i in range(group_pairs)]:
            fetch_queries(pair).start()

            @pl.when(group < short_groups)
            def _():
                fetch_keys(pair, short).start()

            @pl.when(group >= short_groups)
            def _():
                fetch_keys(pair, span).start()

    start(1)
    latent_copy.wait()
    latent_wide[...] = latent_ref[...].astype(jnp.float32)

    def score(row, keys):
        scores = jnp.dot(
            queries_ref[row], held[row, :, :keys], preferred_element_type=jnp.float32
        )
        position = lax.broadcasted_iota(jnp.int32, scores.shape, 1)
        return jnp.where(position < lengths_ref[first_row + row], scores, -jnp.inf)

    def weigh(row, scores):
        fresh = latent_wide[pl.ds(row, 1), :]
        self_score = jnp.sum(
            queries_ref[row].astype(jnp.float32) * fresh, axis=1, keepdims=True
        )
        row_max = jnp.maximum(jnp.max(scores, axis=1, keepdims=True), self_score)
        raised = jnp.exp2((scores - row_max) * exponent_scale)
        self_raised = jnp.exp2((self_score - row_max) * exponent_scale)
        row_total = jnp.sum(raised, axis=1, keepdims=True) + self_raised
        self_weight = self_raised.astype(jnp.bfloat16).astype(jnp.float32)
        return raised.astype(jnp.bfloat16), self_weight, row_total

    def gather(row, keys, weights, self_weight, row_total):
        gathered = lax.dot_general(
            weights,
            held[row, :LAT, :keys],
            (((1,), (1,)), ((), ())),
            preferred_element_type=jnp.float32,
        )
        gathered = gathered + self_weight * latent_wide[pl.ds(row, 1), :LAT]
        return (gathered * (1.0 / row_total)).reshape(owners, owned, LAT)

    def attend_rows(pairs, keys):
        rows = [2 * pair + i for pair in pairs for i in range(2)]
        scored = [score(row, keys) for row in rows]
        weighed = [weigh(row, scores) for row, scores in zip(rows, scored)]
        done = [gather(row, keys, *parts) for row, parts in zip(rows, weighed)]
        size = 2 * owned
        for i, pair in enumerate(pairs):
            out_ref[:, pl.ds(pl.multiple_of(pair * size, size), size), :] = jnp.concatenate(
                done[2 * i : 2 * i + 2], axis=1
            ).astype(jnp.bfloat16)

    def attend_group(group, carry):
        pairs = [order[group * group_pairs + i] for i in range(group_pairs)]
        whole = jnp.logical_or(group == 0, group >= short_groups)
        is_long = jnp.where(group == 0, first_is_long, group >= short_groups)
        for pair in pairs:
            fetch_queries(pair).wait()

            @pl.when(whole)
            def _():
                fetch_keys(pair, span).wait()

            @pl.when(jnp.logical_not(whole))
            def _():
                fetch_keys(pair, short).wait()

        @pl.when(group == 0)
        def _():
            for later in range(2, group_count):
                start(later)

        @pl.when(is_long)
        def _():
            attend_rows(pairs, span)

        @pl.when(jnp.logical_not(is_long))
        def _():
            attend_rows(pairs, short)

        return carry

    lax.fori_loop(0, group_count, attend_group, 0)
    here = lax.axis_index("dp")
    z_size = owners // 2
    for place, owner_ref in enumerate(owner_refs):
        far = (here // z_size + place // z_size) % 2
        owner_ref[...] = out_ref[far * z_size + (here + place) % z_size]


def attend(queries, latent_cache, new_latent, lengths, owners):
    row_count, span, width = latent_cache.shape
    heads = queries.shape[1]
    owned = heads // owners
    vmem = pl.BlockSpec(memory_space=pltpu.VMEM)
    hbm = pl.BlockSpec(memory_space=pltpu.HBM)
    arrays = (lengths, queries, new_latent, jnp.swapaxes(latent_cache, 1, 2))
    return pl.pallas_call(
        attend_kernel,
        out_shape=[jax.ShapeDtypeStruct((row_count * owned, LAT), jnp.bfloat16)] * owners,
        in_specs=[hbm] * len(arrays),
        out_specs=[vmem] * owners,
        scratch_shapes=[
            pltpu.VMEM((owners, row_count * owned, LAT), jnp.bfloat16),
            pltpu.VMEM((row_count, width, span), jnp.bfloat16),
            pltpu.VMEM(queries.shape, jnp.bfloat16),
            pltpu.VMEM(new_latent.shape, jnp.bfloat16),
            pltpu.VMEM(new_latent.shape, jnp.float32),
            pltpu.SMEM(lengths.shape, jnp.int32),
            pltpu.SMEM((row_count // 2,), jnp.int32),
            pltpu.SemaphoreType.DMA((2,)),
            pltpu.SemaphoreType.DMA((row_count // 2,)),
            pltpu.SemaphoreType.DMA((row_count // 2,)),
        ],
        cost_estimate=pl.CostEstimate(
            flops=4 * row_count * heads * span * width,
            bytes_accessed=2 * row_count * span * width,
            transcendentals=row_count * heads * span,
        ),
        compiler_params=pltpu.CompilerParams(vmem_limit_bytes=24 * MIB),
        name="attend",
    )(*(pltpu.with_memory_space_constraint(x, pltpu.HBM) for x in arrays))


def bring_kernel(after_hbm, proj_hbm, proj_ref, arrived):
    del after_hbm
    copy = pltpu.make_async_copy(proj_hbm, proj_ref, arrived)
    copy.start()
    copy.wait()


def bring(output_proj, after):
    return pl.pallas_call(
        bring_kernel,
        out_shape=pltpu.VMEM(output_proj.shape, jnp.bfloat16),
        in_specs=[pl.BlockSpec(memory_space=pl.ANY), pl.BlockSpec(memory_space=pltpu.HBM)],
        out_specs=pl.BlockSpec(memory_space=pltpu.VMEM),
        scratch_shapes=[pltpu.SemaphoreType.DMA],
        cost_estimate=pl.CostEstimate(
            flops=0, bytes_accessed=2 * output_proj.size, transcendentals=0
        ),
        compiler_params=pltpu.CompilerParams(vmem_limit_bytes=16 * MIB),
        name="bring",
    )(after, pltpu.with_memory_space_constraint(output_proj, pltpu.HBM))


def values_kernel(latent_refs, value_up_ref, proj_ref, values_ref, own_ref, send_ref, wide):
    owned, lat, value_size = value_up_ref.shape
    owners, rows_here, columns = 2 * own_ref.shape[0], own_ref.shape[1], own_ref.shape[2]
    rows = owners * rows_here
    z_size = owners // 2

    size = rows_here * owned
    for place, latent_ref in zip((0,) + ORDER, latent_refs):
        far, step = place // z_size, place % z_size
        back = (far * z_size + (z_size - step) % z_size) * size
        for c in range(lat // 128):
            wide[c, back : back + size] = latent_ref[:, c * 128 : (c + 1) * 128].astype(
                jnp.float32
            )
    for h in range(owned):
        mine = jnp.concatenate(
            [wide[c, pl.ds(h, rows, stride=owned), :] for c in range(lat // 128)], axis=1
        ).astype(jnp.bfloat16)
        values_ref[:, h * value_size : (h + 1) * value_size] = jnp.dot(
            mine, value_up_ref[h], preferred_element_type=jnp.float32
        ).astype(jnp.bfloat16)
    flattened = values_ref[...]
    for start in range(0, columns, PROJ_STEP):
        stop = min(start + PROJ_STEP, columns)
        done = jnp.dot(
            flattened,
            proj_ref[:, LEFT_COLUMNS + start : LEFT_COLUMNS + stop],
            preferred_element_type=jnp.float32,
        ).astype(jnp.bfloat16)
        done = done.reshape(2, z_size, rows_here, stop - start)
        own_ref[:, :, start:stop] = done[0]
        send_ref[:, :, start:stop] = done[1]


def make_values(owned_latents, value_up, output_proj, owners, rows_here):
    owned, lat, value_size = value_up.shape
    depth, width = output_proj.shape
    columns = width - LEFT_COLUMNS
    rows = owners * rows_here
    vmem = pl.BlockSpec(memory_space=pltpu.VMEM)
    half = jax.ShapeDtypeStruct((owners // 2, rows_here, columns), jnp.bfloat16)
    return pl.pallas_call(
        values_kernel,
        out_shape=(jax.ShapeDtypeStruct((rows, owned * value_size), jnp.bfloat16), half, half),
        in_specs=[[vmem] * owners, vmem, vmem],
        out_specs=(vmem, vmem, vmem),
        scratch_shapes=[pltpu.VMEM((lat // 128, rows * owned, 128), jnp.float32)],
        cost_estimate=pl.CostEstimate(
            flops=2 * rows * depth * columns, bytes_accessed=2 * depth * columns, transcendentals=0
        ),
        compiler_params=pltpu.CompilerParams(vmem_limit_bytes=20 * MIB),
        name="values",
    )(owned_latents, value_up, pltpu.with_memory_space_constraint(output_proj, pltpu.VMEM))


def project_kernel(values_ref, proj_ref, *out_refs):
    rows_here, columns = out_refs[0].shape[1:]
    z_size = len(out_refs)
    flattened = values_ref[...]
    for start in range(0, columns, PROJ_STEP):
        stop = min(start + PROJ_STEP, columns)
        done = jnp.dot(
            flattened, proj_ref[:, start:stop], preferred_element_type=jnp.float32
        ).astype(jnp.bfloat16)
        done = done.reshape(2, z_size, rows_here, stop - start)
        for step in range(z_size):
            out_refs[step][:, :, start:stop] = done[:, step]


def project(values, output_proj, owners, rows_here):
    rows, depth = values.shape
    columns = LEFT_COLUMNS
    z_size = owners // 2
    vmem = pl.BlockSpec(memory_space=pltpu.VMEM)
    part = jax.ShapeDtypeStruct((2, rows_here, columns), jnp.bfloat16)
    return pl.pallas_call(
        project_kernel,
        out_shape=[part] * z_size,
        in_specs=[vmem, vmem],
        out_specs=[vmem] * z_size,
        cost_estimate=pl.CostEstimate(
            flops=2 * rows * depth * columns, bytes_accessed=2 * depth * columns, transcendentals=0
        ),
        compiler_params=pltpu.CompilerParams(vmem_limit_bytes=20 * MIB),
        name="project",
    )(values, pltpu.with_memory_space_constraint(output_proj, pltpu.VMEM))


def add_far_kernel(own_ref, came_ref, *out_refs):
    for step, out_ref in enumerate(out_refs, 1):
        both = own_ref[step].astype(jnp.float32) + came_ref[step].astype(jnp.float32)
        out_ref[...] = both.astype(jnp.bfloat16)


def add_far(own, came):
    vmem = pl.BlockSpec(memory_space=pltpu.VMEM)
    return pl.pallas_call(
        add_far_kernel,
        out_shape=[jax.ShapeDtypeStruct(own.shape[1:], jnp.bfloat16)] * (own.shape[0] - 1),
        in_specs=[vmem, vmem],
        out_specs=[vmem] * (own.shape[0] - 1),
        cost_estimate=pl.CostEstimate(flops=own.size, bytes_accessed=own.size * 6, transcendentals=0),
        compiler_params=pltpu.CompilerParams(vmem_limit_bytes=16 * MIB),
        name="add_far",
    )(own, came)


def add_near_kernel(*refs):
    *part_refs, out_ref = refs
    total = part_refs[0][1].astype(jnp.float32)
    for part_ref in part_refs[1:]:
        total = total + part_ref[1].astype(jnp.float32)
    out_ref[...] = total.astype(jnp.bfloat16)


def add_near(parts):
    vmem = pl.BlockSpec(memory_space=pltpu.VMEM)
    return pl.pallas_call(
        add_near_kernel,
        out_shape=jax.ShapeDtypeStruct(parts[0].shape[1:], jnp.bfloat16),
        in_specs=[vmem] * len(parts),
        out_specs=vmem,
        cost_estimate=pl.CostEstimate(
            flops=parts[0].size * 2, bytes_accessed=parts[0].size * 8, transcendentals=0
        ),
        compiler_params=pltpu.CompilerParams(vmem_limit_bytes=16 * MIB),
        name="add_near",
    )(*parts)


def finish_kernel(near_refs, far_ref, own_ref, came_ref, step_refs, residual_ref, gain_ref,
                  hidden_ref, normed_ref):
    rows, first = far_ref.shape
    width = residual_ref.shape[1]
    left = residual_ref[:, :first].astype(jnp.float32) + far_ref[...].astype(jnp.float32)
    for near_ref in near_refs:
        left = left + near_ref[0].astype(jnp.float32)
    right = residual_ref[:, first:].astype(jnp.float32) + (
        own_ref[0].astype(jnp.float32) + came_ref[0].astype(jnp.float32)
    )
    for step_ref in step_refs:
        right = right + step_ref[...].astype(jnp.float32)
    total = jnp.sum(left * left, axis=1, keepdims=True) + jnp.sum(
        right * right, axis=1, keepdims=True
    )
    inverse_rms = lax.rsqrt(total * (1.0 / width) + norm_eps)
    for part, here in ((left, slice(0, first)), (right, slice(first, width))):
        hidden_ref[:, here] = part.astype(jnp.bfloat16)
        normed = part * inverse_rms * gain_ref[:, here].astype(jnp.float32)
        normed_ref[:, here] = normed.astype(jnp.bfloat16)


def finish(nears, far, own, came, steps, residual, norm_gain):
    vmem = pl.BlockSpec(memory_space=pltpu.VMEM)
    shape = jax.ShapeDtypeStruct(residual.shape, jnp.bfloat16)
    return pl.pallas_call(
        finish_kernel,
        out_shape=(shape, shape),
        in_specs=[[vmem] * len(nears), vmem, vmem, vmem, [vmem] * len(steps), vmem, vmem],
        out_specs=(vmem, vmem),
        compiler_params=pltpu.CompilerParams(vmem_limit_bytes=32 * MIB),
        name="finish",
    )(nears, far, own, came, steps, residual, norm_gain.reshape(1, -1))


def send(array, far, step, mesh_shape):
    replicas, owners = mesh_shape
    z_size = owners // 2
    pairs = []
    for replica in range(replicas):
        for owner in range(owners):
            to_replica = (replica + far * (replicas // 2)) % replicas
            to_half = (owner // z_size + far) % 2
            to_owner = to_half * z_size + (owner + step) % z_size
            pairs.append((replica * owners + owner, to_replica * owners + to_owner))
    return lax.ppermute(array, ("rep", "dp"), pairs)


def per_device(
    queries, latent_cache, new_latent, lengths, value_up, output_proj, residual, norm_gain
):
    owners = lax.axis_size("dp")
    mesh_shape = (lax.axis_size("rep"), owners)
    rows_here = latent_cache.shape[0]
    z_size = owners // 2
    latents = attend(queries, latent_cache, new_latent, lengths, owners)
    owned_latents = [latents[0]] + [
        send(latents[place], place // z_size, place % z_size, mesh_shape)
        for place in ORDER
    ]
    proj_near = bring(output_proj, latents[0])
    values, own, across = make_values(owned_latents, value_up, proj_near, owners, rows_here)
    came = send(across, 1, 0, mesh_shape)
    parts = project(values, proj_near, owners, rows_here)
    nears = [parts[0]] + [send(parts[k], 0, k, mesh_shape) for k in range(1, z_size)]
    pairs = add_far(own, came)
    steps = [send(pair, 0, k, mesh_shape) for k, pair in enumerate(pairs, 1)]
    far = send(add_near(nears), 1, 0, mesh_shape)
    return finish(nears, far, own, came, steps, residual, norm_gain)


def solution(mesh):
    return jax.shard_map(
        per_device,
        mesh=mesh,
        in_specs=(
            P(("rep", "dp"), None, None),
            P(("rep", "dp"), None, None),
            P(("rep", "dp"), None),
            P("rep"),
            P("dp", None, None),
            P("dp", None),
            P(("rep", "dp"), None),
            P(),
        ),
        out_specs=(P(("rep", "dp"), None), P(("rep", "dp"), None)),
        check_vma=False,
    )
```

```python
import jax
import jax.numpy as jnp
from jax import lax
from jax.experimental import pallas as pl
from jax.experimental.pallas import tpu as pltpu
from jax.sharding import PartitionSpec as P

LAT = 512
GROUP_ROWS = 4
PROJ_STEP = 1024
LEFT_COLUMNS = 3456
ORDERS = ((6, 5, 7, 4, 2, 1, 3), (6, 5, 7, 4, 2, 1, 3))
exponent_scale = 192.0 ** (-0.5) * 1.4426950408889634
norm_eps = 1e-06
MIB = 1024 * 1024


def attend_kernel(
    lengths_hbm, queries_hbm, latent_hbm, cache_hbm, *refs
):
    *owner_refs, out_ref = refs[:-9]
    (
        held, queries_ref, latent_ref, latent_wide,
        lengths_ref, order, arrived_small, arrived_queries, arrived_keys,
    ) = refs[-9:]
    row_count, width, span = held.shape
    owners, _, _ = out_ref.shape
    heads = queries_ref.shape[1]
    owned = heads // owners
    first_row = lax.axis_index("dp") * row_count
    pair_count = row_count // 2
    group_pairs = GROUP_ROWS // 2
    group_count = pair_count // group_pairs
    short = span // 2

    lengths_copy = pltpu.make_async_copy(lengths_hbm, lengths_ref, arrived_small.at[0])
    latent_copy = pltpu.make_async_copy(latent_hbm, latent_ref, arrived_small.at[1])

    def fetch_queries(pair):
        rows = pl.ds(2 * pair, 2)
        return pltpu.make_async_copy(
            queries_hbm.at[rows], queries_ref.at[rows], arrived_queries.at[pair]
        )

    def fetch_keys(pair, keys):
        rows = pl.ds(2 * pair, 2)
        return pltpu.make_async_copy(
            cache_hbm.at[rows, :, pl.ds(0, keys)],
            held.at[rows, :, pl.ds(0, keys)],
            arrived_keys.at[pair],
        )

    for pair in range(group_pairs):
        order[pair] = pair
        fetch_queries(pair).start()
        fetch_keys(pair, span).start()
    lengths_copy.start()
    latent_copy.start()
    lengths_copy.wait()
    longest = [
        jnp.maximum(lengths_ref[first_row + 2 * pair], lengths_ref[first_row + 2 * pair + 1])
        for pair in range(pair_count)
    ]
    is_long = [(length > short).astype(jnp.int32) for length in longest]

    short_slot = group_pairs
    long_slot = pair_count - sum(is_long[group_pairs:])
    first_is_long = sum(is_long[:group_pairs]) > 0
    short_groups = long_slot // group_pairs
    for pair in range(group_pairs, pair_count):
        order[jnp.where(is_long[pair] == 1, long_slot, short_slot)] = pair
        long_slot = long_slot + is_long[pair]
        short_slot = short_slot + 1 - is_long[pair]

    def start(group):
        for pair in [order[group * group_pairs + i] for i in range(group_pairs)]:
            fetch_queries(pair).start()

            @pl.when(group < short_groups)
            def _():
                fetch_keys(pair, short).start()

            @pl.when(group >= short_groups)
            def _():
                fetch_keys(pair, span).start()

    start(1)
    latent_copy.wait()
    latent_wide[...] = latent_ref[...].astype(jnp.float32)

    def score(row, keys):
        scores = jnp.dot(
            queries_ref[row], held[row, :, :keys], preferred_element_type=jnp.float32
        )
        position = lax.broadcasted_iota(jnp.int32, scores.shape, 1)
        return jnp.where(position < lengths_ref[first_row + row], scores, -jnp.inf)

    def weigh(row, scores):
        fresh = latent_wide[pl.ds(row, 1), :]
        self_score = jnp.sum(
            queries_ref[row].astype(jnp.float32) * fresh, axis=1, keepdims=True
        )
        row_max = jnp.maximum(jnp.max(scores, axis=1, keepdims=True), self_score)
        raised = jnp.exp2((scores - row_max) * exponent_scale)
        self_raised = jnp.exp2((self_score - row_max) * exponent_scale)
        row_total = jnp.sum(raised, axis=1, keepdims=True) + self_raised
        self_weight = self_raised.astype(jnp.bfloat16).astype(jnp.float32)
        return raised.astype(jnp.bfloat16), self_weight, row_total

    def gather(row, keys, weights, self_weight, row_total):
        gathered = lax.dot_general(
            weights,
            held[row, :LAT, :keys],
            (((1,), (1,)), ((), ())),
            preferred_element_type=jnp.float32,
        )
        gathered = gathered + self_weight * latent_wide[pl.ds(row, 1), :LAT]
        return (gathered * (1.0 / row_total)).reshape(owners, owned, LAT)

    def attend_rows(pairs, keys):
        rows = [2 * pair + i for pair in pairs for i in range(2)]
        scored = [score(row, keys) for row in rows]
        weighed = [weigh(row, scores) for row, scores in zip(rows, scored)]
        done = [gather(row, keys, *parts) for row, parts in zip(rows, weighed)]
        size = 2 * owned
        for i, pair in enumerate(pairs):
            out_ref[:, pl.ds(pl.multiple_of(pair * size, size), size), :] = jnp.concatenate(
                done[2 * i : 2 * i + 2], axis=1
            ).astype(jnp.bfloat16)

    def attend_group(group, carry):
        pairs = [order[group * group_pairs + i] for i in range(group_pairs)]
        whole = jnp.logical_or(group == 0, group >= short_groups)
        is_long = jnp.where(group == 0, first_is_long, group >= short_groups)
        for pair in pairs:
            fetch_queries(pair).wait()

            @pl.when(whole)
            def _():
                fetch_keys(pair, span).wait()

            @pl.when(jnp.logical_not(whole))
            def _():
                fetch_keys(pair, short).wait()

        @pl.when(group == 0)
        def _():
            for later in range(2, group_count):
                start(later)

        @pl.when(is_long)
        def _():
            attend_rows(pairs, span)

        @pl.when(jnp.logical_not(is_long))
        def _():
            attend_rows(pairs, short)

        return carry

    lax.fori_loop(0, group_count, attend_group, 0)
    here = lax.axis_index("dp")
    core = lax.axis_index("rep") % 2
    z_size = owners // 2
    for owner_ref, places in zip(owner_refs, ((0, 0),) + tuple(zip(*ORDERS))):
        place = jnp.where(core == 0, *places)
        far = (here // z_size + place // z_size) % 2
        step = jnp.where(core == 0, place, z_size - place % z_size)
        owner_ref[...] = out_ref[far * z_size + (here + step) % z_size]


def attend(queries, latent_cache, new_latent, lengths, owners):
    row_count, span, width = latent_cache.shape
    heads = queries.shape[1]
    owned = heads // owners
    vmem = pl.BlockSpec(memory_space=pltpu.VMEM)
    hbm = pl.BlockSpec(memory_space=pltpu.HBM)
    arrays = (lengths, queries, new_latent, jnp.swapaxes(latent_cache, 1, 2))
    return pl.pallas_call(
        attend_kernel,
        out_shape=[jax.ShapeDtypeStruct((row_count * owned, LAT), jnp.bfloat16)] * owners,
        in_specs=[hbm] * len(arrays),
        out_specs=[vmem] * owners,
        scratch_shapes=[
            pltpu.VMEM((owners, row_count * owned, LAT), jnp.bfloat16),
            pltpu.VMEM((row_count, width, span), jnp.bfloat16),
            pltpu.VMEM(queries.shape, jnp.bfloat16),
            pltpu.VMEM(new_latent.shape, jnp.bfloat16),
            pltpu.VMEM(new_latent.shape, jnp.float32),
            pltpu.SMEM(lengths.shape, jnp.int32),
            pltpu.SMEM((row_count // 2,), jnp.int32),
            pltpu.SemaphoreType.DMA((2,)),
            pltpu.SemaphoreType.DMA((row_count // 2,)),
            pltpu.SemaphoreType.DMA((row_count // 2,)),
        ],
        cost_estimate=pl.CostEstimate(
            flops=4 * row_count * heads * span * width,
            bytes_accessed=2 * row_count * span * width,
            transcendentals=row_count * heads * span,
        ),
        compiler_params=pltpu.CompilerParams(vmem_limit_bytes=24 * MIB),
        name="attend",
    )(*(pltpu.with_memory_space_constraint(x, pltpu.HBM) for x in arrays))


def bring_kernel(after_hbm, proj_hbm, proj_ref, arrived):
    del after_hbm
    copy = pltpu.make_async_copy(proj_hbm, proj_ref, arrived)
    copy.start()
    copy.wait()


def bring(output_proj, after):
    return pl.pallas_call(
        bring_kernel,
        out_shape=pltpu.VMEM(output_proj.shape, jnp.bfloat16),
        in_specs=[pl.BlockSpec(memory_space=pl.ANY), pl.BlockSpec(memory_space=pltpu.HBM)],
        out_specs=pl.BlockSpec(memory_space=pltpu.VMEM),
        scratch_shapes=[pltpu.SemaphoreType.DMA],
        cost_estimate=pl.CostEstimate(
            flops=0, bytes_accessed=2 * output_proj.size, transcendentals=0
        ),
        compiler_params=pltpu.CompilerParams(vmem_limit_bytes=16 * MIB),
        name="bring",
    )(after, pltpu.with_memory_space_constraint(output_proj, pltpu.HBM))


def values_kernel(latent_refs, value_up_ref, proj_ref, values_ref, own_ref, send_ref, wide):
    owned, lat, value_size = value_up_ref.shape
    owners, rows_here, columns = 2 * own_ref.shape[0], own_ref.shape[1], own_ref.shape[2]
    rows = owners * rows_here
    z_size = owners // 2

    size = rows_here * owned
    core = lax.axis_index("rep") % 2
    for latent_ref, places in zip(latent_refs, ((0, 0),) + tuple(zip(*ORDERS))):
        place = jnp.where(core == 0, *places)
        step = (z_size - place % z_size) % z_size
        back = pl.multiple_of((place // z_size * z_size + step) * size, size)
        for c in range(lat // 128):
            wide[c, pl.ds(back, size)] = latent_ref[:, c * 128 : (c + 1) * 128].astype(
                jnp.float32
            )
    for h in range(owned):
        mine = jnp.concatenate(
            [wide[c, pl.ds(h, rows, stride=owned), :] for c in range(lat // 128)], axis=1
        ).astype(jnp.bfloat16)
        values_ref[:, h * value_size : (h + 1) * value_size] = jnp.dot(
            mine, value_up_ref[h], preferred_element_type=jnp.float32
        ).astype(jnp.bfloat16)
    flattened = values_ref[...]
    for start in range(0, columns, PROJ_STEP):
        stop = min(start + PROJ_STEP, columns)
        done = jnp.dot(
            flattened,
            proj_ref[:, LEFT_COLUMNS + start : LEFT_COLUMNS + stop],
            preferred_element_type=jnp.float32,
        ).astype(jnp.bfloat16)
        done = done.reshape(2, z_size, rows_here, stop - start)
        own_ref[:, :, start:stop] = done[0]
        send_ref[:, :, start:stop] = done[1]


def make_values(owned_latents, value_up, output_proj, owners, rows_here):
    owned, lat, value_size = value_up.shape
    depth, width = output_proj.shape
    columns = width - LEFT_COLUMNS
    rows = owners * rows_here
    vmem = pl.BlockSpec(memory_space=pltpu.VMEM)
    half = jax.ShapeDtypeStruct((owners // 2, rows_here, columns), jnp.bfloat16)
    return pl.pallas_call(
        values_kernel,
        out_shape=(jax.ShapeDtypeStruct((rows, owned * value_size), jnp.bfloat16), half, half),
        in_specs=[[vmem] * owners, vmem, vmem],
        out_specs=(vmem, vmem, vmem),
        scratch_shapes=[pltpu.VMEM((lat // 128, rows * owned, 128), jnp.float32)],
        cost_estimate=pl.CostEstimate(
            flops=2 * rows * depth * columns, bytes_accessed=2 * depth * columns, transcendentals=0
        ),
        compiler_params=pltpu.CompilerParams(vmem_limit_bytes=20 * MIB),
        name="values",
    )(owned_latents, value_up, pltpu.with_memory_space_constraint(output_proj, pltpu.VMEM))


def project_kernel(values_ref, proj_ref, *out_refs):
    rows_here, columns = out_refs[0].shape[1:]
    z_size = len(out_refs)
    flattened = values_ref[...]
    for start in range(0, columns, PROJ_STEP):
        stop = min(start + PROJ_STEP, columns)
        done = jnp.dot(
            flattened, proj_ref[:, start:stop], preferred_element_type=jnp.float32
        ).astype(jnp.bfloat16)
        done = done.reshape(2, z_size, rows_here, stop - start)
        for step in range(z_size):
            out_refs[step][:, :, start:stop] = done[:, step]


def project(values, output_proj, owners, rows_here):
    rows, depth = values.shape
    columns = LEFT_COLUMNS
    z_size = owners // 2
    vmem = pl.BlockSpec(memory_space=pltpu.VMEM)
    part = jax.ShapeDtypeStruct((2, rows_here, columns), jnp.bfloat16)
    return pl.pallas_call(
        project_kernel,
        out_shape=[part] * z_size,
        in_specs=[vmem, vmem],
        out_specs=[vmem] * z_size,
        cost_estimate=pl.CostEstimate(
            flops=2 * rows * depth * columns, bytes_accessed=2 * depth * columns, transcendentals=0
        ),
        compiler_params=pltpu.CompilerParams(vmem_limit_bytes=20 * MIB),
        name="project",
    )(values, pltpu.with_memory_space_constraint(output_proj, pltpu.VMEM))


def add_far_kernel(own_ref, came_ref, *out_refs):
    for step, out_ref in enumerate(out_refs, 1):
        both = own_ref[step].astype(jnp.float32) + came_ref[step].astype(jnp.float32)
        out_ref[...] = both.astype(jnp.bfloat16)


def add_far(own, came):
    vmem = pl.BlockSpec(memory_space=pltpu.VMEM)
    return pl.pallas_call(
        add_far_kernel,
        out_shape=[jax.ShapeDtypeStruct(own.shape[1:], jnp.bfloat16)] * (own.shape[0] - 1),
        in_specs=[vmem, vmem],
        out_specs=[vmem] * (own.shape[0] - 1),
        cost_estimate=pl.CostEstimate(flops=own.size, bytes_accessed=own.size * 6, transcendentals=0),
        compiler_params=pltpu.CompilerParams(vmem_limit_bytes=16 * MIB),
        name="add_far",
    )(own, came)


def add_near_kernel(*refs):
    *part_refs, out_ref = refs
    total = part_refs[0][1].astype(jnp.float32)
    for part_ref in part_refs[1:]:
        total = total + part_ref[1].astype(jnp.float32)
    out_ref[...] = total.astype(jnp.bfloat16)


def add_near(parts):
    vmem = pl.BlockSpec(memory_space=pltpu.VMEM)
    return pl.pallas_call(
        add_near_kernel,
        out_shape=jax.ShapeDtypeStruct(parts[0].shape[1:], jnp.bfloat16),
        in_specs=[vmem] * len(parts),
        out_specs=vmem,
        cost_estimate=pl.CostEstimate(
            flops=parts[0].size * 2, bytes_accessed=parts[0].size * 8, transcendentals=0
        ),
        compiler_params=pltpu.CompilerParams(vmem_limit_bytes=16 * MIB),
        name="add_near",
    )(*parts)


def finish_kernel(near_refs, far_ref, own_ref, came_ref, step_refs, residual_ref, gain_ref,
                  hidden_ref, normed_ref):
    rows, first = far_ref.shape
    width = residual_ref.shape[1]
    left = residual_ref[:, :first].astype(jnp.float32) + far_ref[...].astype(jnp.float32)
    for near_ref in near_refs:
        left = left + near_ref[0].astype(jnp.float32)
    right = residual_ref[:, first:].astype(jnp.float32) + (
        own_ref[0].astype(jnp.float32) + came_ref[0].astype(jnp.float32)
    )
    for step_ref in step_refs:
        right = right + step_ref[...].astype(jnp.float32)
    total = jnp.sum(left * left, axis=1, keepdims=True) + jnp.sum(
        right * right, axis=1, keepdims=True
    )
    inverse_rms = lax.rsqrt(total * (1.0 / width) + norm_eps)
    for part, here in ((left, slice(0, first)), (right, slice(first, width))):
        hidden_ref[:, here] = part.astype(jnp.bfloat16)
        normed = part * inverse_rms * gain_ref[:, here].astype(jnp.float32)
        normed_ref[:, here] = normed.astype(jnp.bfloat16)


def finish(nears, far, own, came, steps, residual, norm_gain):
    vmem = pl.BlockSpec(memory_space=pltpu.VMEM)
    shape = jax.ShapeDtypeStruct(residual.shape, jnp.bfloat16)
    return pl.pallas_call(
        finish_kernel,
        out_shape=(shape, shape),
        in_specs=[[vmem] * len(nears), vmem, vmem, vmem, [vmem] * len(steps), vmem, vmem],
        out_specs=(vmem, vmem),
        compiler_params=pltpu.CompilerParams(vmem_limit_bytes=32 * MIB),
        name="finish",
    )(nears, far, own, came, steps, residual, norm_gain.reshape(1, -1))


def send(array, places, mesh_shape):
    replicas, owners = mesh_shape
    z_size = owners // 2
    pairs = []
    for replica in range(replicas):
        far, step = divmod(places[replica % 2], z_size)
        step = -step if replica % 2 else step
        for owner in range(owners):
            to_replica = (replica + far * (replicas // 2)) % replicas
            to_half = (owner // z_size + far) % 2
            to_owner = to_half * z_size + (owner + step) % z_size
            pairs.append((replica * owners + owner, to_replica * owners + to_owner))
    return lax.ppermute(array, ("rep", "dp"), pairs)


def per_device(
    queries, latent_cache, new_latent, lengths, value_up, output_proj, residual, norm_gain
):
    owners = lax.axis_size("dp")
    mesh_shape = (lax.axis_size("rep"), owners)
    rows_here = latent_cache.shape[0]
    z_size = owners // 2
    latents = attend(queries, latent_cache, new_latent, lengths, owners)
    owned_latents = [latents[0]] + [
        send(latent, places, mesh_shape) for latent, places in zip(latents[1:], zip(*ORDERS))
    ]
    proj_near = bring(output_proj, latents[0])
    values, own, across = make_values(owned_latents, value_up, proj_near, owners, rows_here)
    came = send(across, (z_size, z_size), mesh_shape)
    parts = project(values, proj_near, owners, rows_here)
    nears = [parts[0]] + [send(parts[k], (k, k), mesh_shape) for k in range(1, z_size)]
    pairs = add_far(own, came)
    steps = [send(pair, (k, k), mesh_shape) for k, pair in enumerate(pairs, 1)]
    far = send(add_near(nears), (z_size, z_size), mesh_shape)
    return finish(nears, far, own, came, steps, residual, norm_gain)


def solution(mesh):
    return jax.shard_map(
        per_device,
        mesh=mesh,
        in_specs=(
            P(("rep", "dp"), None, None),
            P(("rep", "dp"), None, None),
            P(("rep", "dp"), None),
            P("rep"),
            P("dp", None, None),
            P("dp", None),
            P(("rep", "dp"), None),
            P(),
        ),
        out_specs=(P(("rep", "dp"), None), P(("rep", "dp"), None)),
        check_vma=False,
    )
```

```python
import jax
import jax.numpy as jnp
from jax import lax
from jax.experimental import pallas as pl
from jax.experimental.pallas import tpu as pltpu
from jax.sharding import PartitionSpec as P

LAT = 512
GROUP_ROWS = 4
PROJ_STEP = 1024
LEFT_COLUMNS = 3456
Z_ORDER = (1, 3, 2)
ORDERS = ((6, 5, 7, 4, 2, 1, 3), (6, 5, 7, 4, 2, 1, 3))
exponent_scale = 192.0 ** (-0.5) * 1.4426950408889634
norm_eps = 1e-06
MIB = 1024 * 1024


def attend_kernel(
    lengths_hbm, queries_hbm, latent_hbm, cache_hbm, *refs
):
    *owner_refs, out_ref = refs[:-9]
    (
        held, queries_ref, latent_ref, latent_wide,
        lengths_ref, order, arrived_small, arrived_queries, arrived_keys,
    ) = refs[-9:]
    row_count, width, span = held.shape
    owners, _, _ = out_ref.shape
    heads = queries_ref.shape[1]
    owned = heads // owners
    first_row = lax.axis_index("dp") * row_count
    pair_count = row_count // 2
    group_pairs = GROUP_ROWS // 2
    group_count = pair_count // group_pairs
    short = span // 2

    lengths_copy = pltpu.make_async_copy(lengths_hbm, lengths_ref, arrived_small.at[0])
    latent_copy = pltpu.make_async_copy(latent_hbm, latent_ref, arrived_small.at[1])

    def fetch_queries(pair):
        rows = pl.ds(2 * pair, 2)
        return pltpu.make_async_copy(
            queries_hbm.at[rows], queries_ref.at[rows], arrived_queries.at[pair]
        )

    def fetch_keys(pair, keys):
        rows = pl.ds(2 * pair, 2)
        return pltpu.make_async_copy(
            cache_hbm.at[rows, :, pl.ds(0, keys)],
            held.at[rows, :, pl.ds(0, keys)],
            arrived_keys.at[pair],
        )

    for pair in range(group_pairs):
        order[pair] = pair
        fetch_queries(pair).start()
        fetch_keys(pair, span).start()
    lengths_copy.start()
    latent_copy.start()
    lengths_copy.wait()
    longest = [
        jnp.maximum(lengths_ref[first_row + 2 * pair], lengths_ref[first_row + 2 * pair + 1])
        for pair in range(pair_count)
    ]
    is_long = [(length > short).astype(jnp.int32) for length in longest]

    short_slot = group_pairs
    long_slot = pair_count - sum(is_long[group_pairs:])
    first_is_long = sum(is_long[:group_pairs]) > 0
    short_groups = long_slot // group_pairs
    for pair in range(group_pairs, pair_count):
        order[jnp.where(is_long[pair] == 1, long_slot, short_slot)] = pair
        long_slot = long_slot + is_long[pair]
        short_slot = short_slot + 1 - is_long[pair]

    def start(group):
        for pair in [order[group * group_pairs + i] for i in range(group_pairs)]:
            fetch_queries(pair).start()

            @pl.when(group < short_groups)
            def _():
                fetch_keys(pair, short).start()

            @pl.when(group >= short_groups)
            def _():
                fetch_keys(pair, span).start()

    start(1)
    latent_copy.wait()
    latent_wide[...] = latent_ref[...].astype(jnp.float32)

    def score(row, keys):
        scores = jnp.dot(
            queries_ref[row], held[row, :, :keys], preferred_element_type=jnp.float32
        )
        position = lax.broadcasted_iota(jnp.int32, scores.shape, 1)
        return jnp.where(position < lengths_ref[first_row + row], scores, -jnp.inf)

    def weigh(row, scores):
        fresh = latent_wide[pl.ds(row, 1), :]
        self_score = jnp.sum(
            queries_ref[row].astype(jnp.float32) * fresh, axis=1, keepdims=True
        )
        row_max = jnp.maximum(jnp.max(scores, axis=1, keepdims=True), self_score)
        raised = jnp.exp2((scores - row_max) * exponent_scale)
        self_raised = jnp.exp2((self_score - row_max) * exponent_scale)
        row_total = jnp.sum(raised, axis=1, keepdims=True) + self_raised
        self_weight = self_raised.astype(jnp.bfloat16).astype(jnp.float32)
        return raised.astype(jnp.bfloat16), self_weight, row_total

    def gather(row, keys, weights, self_weight, row_total):
        gathered = lax.dot_general(
            weights,
            held[row, :LAT, :keys],
            (((1,), (1,)), ((), ())),
            preferred_element_type=jnp.float32,
        )
        gathered = gathered + self_weight * latent_wide[pl.ds(row, 1), :LAT]
        return (gathered * (1.0 / row_total)).reshape(owners, owned, LAT)

    def attend_rows(pairs, keys):
        rows = [2 * pair + i for pair in pairs for i in range(2)]
        scored = [score(row, keys) for row in rows]
        weighed = [weigh(row, scores) for row, scores in zip(rows, scored)]
        done = [gather(row, keys, *parts) for row, parts in zip(rows, weighed)]
        size = 2 * owned
        for i, pair in enumerate(pairs):
            out_ref[:, pl.ds(pl.multiple_of(pair * size, size), size), :] = jnp.concatenate(
                done[2 * i : 2 * i + 2], axis=1
            ).astype(jnp.bfloat16)

    def attend_group(group, carry):
        pairs = [order[group * group_pairs + i] for i in range(group_pairs)]
        whole = jnp.logical_or(group == 0, group >= short_groups)
        is_long = jnp.where(group == 0, first_is_long, group >= short_groups)
        for pair in pairs:
            fetch_queries(pair).wait()

            @pl.when(whole)
            def _():
                fetch_keys(pair, span).wait()

            @pl.when(jnp.logical_not(whole))
            def _():
                fetch_keys(pair, short).wait()

        @pl.when(group == 0)
        def _():
            for later in range(2, group_count):
                start(later)

        @pl.when(is_long)
        def _():
            attend_rows(pairs, span)

        @pl.when(jnp.logical_not(is_long))
        def _():
            attend_rows(pairs, short)

        return carry

    lax.fori_loop(0, group_count, attend_group, 0)
    here = lax.axis_index("dp")
    core = lax.axis_index("rep") % 2
    z_size = owners // 2
    for owner_ref, places in zip(owner_refs, ((0, 0),) + tuple(zip(*ORDERS))):
        place = jnp.where(core == 0, *places)
        far = (here // z_size + place // z_size) % 2
        step = jnp.where(core == 0, place, z_size - place % z_size)
        owner_ref[...] = out_ref[far * z_size + (here + step) % z_size]


def attend(queries, latent_cache, new_latent, lengths, owners):
    row_count, span, width = latent_cache.shape
    heads = queries.shape[1]
    owned = heads // owners
    vmem = pl.BlockSpec(memory_space=pltpu.VMEM)
    hbm = pl.BlockSpec(memory_space=pltpu.HBM)
    arrays = (lengths, queries, new_latent, jnp.swapaxes(latent_cache, 1, 2))
    return pl.pallas_call(
        attend_kernel,
        out_shape=[jax.ShapeDtypeStruct((row_count * owned, LAT), jnp.bfloat16)] * owners,
        in_specs=[hbm] * len(arrays),
        out_specs=[vmem] * owners,
        scratch_shapes=[
            pltpu.VMEM((owners, row_count * owned, LAT), jnp.bfloat16),
            pltpu.VMEM((row_count, width, span), jnp.bfloat16),
            pltpu.VMEM(queries.shape, jnp.bfloat16),
            pltpu.VMEM(new_latent.shape, jnp.bfloat16),
            pltpu.VMEM(new_latent.shape, jnp.float32),
            pltpu.SMEM(lengths.shape, jnp.int32),
            pltpu.SMEM((row_count // 2,), jnp.int32),
            pltpu.SemaphoreType.DMA((2,)),
            pltpu.SemaphoreType.DMA((row_count // 2,)),
            pltpu.SemaphoreType.DMA((row_count // 2,)),
        ],
        cost_estimate=pl.CostEstimate(
            flops=4 * row_count * heads * span * width,
            bytes_accessed=2 * row_count * span * width,
            transcendentals=row_count * heads * span,
        ),
        compiler_params=pltpu.CompilerParams(vmem_limit_bytes=24 * MIB),
        name="attend",
    )(*(pltpu.with_memory_space_constraint(x, pltpu.HBM) for x in arrays))


def bring_kernel(after_hbm, proj_hbm, proj_ref, arrived):
    del after_hbm
    copy = pltpu.make_async_copy(proj_hbm, proj_ref, arrived)
    copy.start()
    copy.wait()


def bring(output_proj, after):
    return pl.pallas_call(
        bring_kernel,
        out_shape=pltpu.VMEM(output_proj.shape, jnp.bfloat16),
        in_specs=[pl.BlockSpec(memory_space=pl.ANY), pl.BlockSpec(memory_space=pltpu.HBM)],
        out_specs=pl.BlockSpec(memory_space=pltpu.VMEM),
        scratch_shapes=[pltpu.SemaphoreType.DMA],
        cost_estimate=pl.CostEstimate(
            flops=0, bytes_accessed=2 * output_proj.size, transcendentals=0
        ),
        compiler_params=pltpu.CompilerParams(vmem_limit_bytes=16 * MIB),
        name="bring",
    )(after, pltpu.with_memory_space_constraint(output_proj, pltpu.HBM))


def values_kernel(latent_refs, value_up_ref, proj_ref, values_ref, own_ref, send_ref, wide):
    owned, lat, value_size = value_up_ref.shape
    owners, rows_here, columns = 2 * own_ref.shape[0], own_ref.shape[1], own_ref.shape[2]
    rows = owners * rows_here
    z_size = owners // 2

    size = rows_here * owned
    core = lax.axis_index("rep") % 2
    for latent_ref, places in zip(latent_refs, ((0, 0),) + tuple(zip(*ORDERS))):
        place = jnp.where(core == 0, *places)
        step = (z_size - place % z_size) % z_size
        back = pl.multiple_of((place // z_size * z_size + step) * size, size)
        for c in range(lat // 128):
            wide[c, pl.ds(back, size)] = latent_ref[:, c * 128 : (c + 1) * 128].astype(
                jnp.float32
            )
    for h in range(owned):
        mine = jnp.concatenate(
            [wide[c, pl.ds(h, rows, stride=owned), :] for c in range(lat // 128)], axis=1
        ).astype(jnp.bfloat16)
        values_ref[:, h * value_size : (h + 1) * value_size] = jnp.dot(
            mine, value_up_ref[h], preferred_element_type=jnp.float32
        ).astype(jnp.bfloat16)
    flattened = values_ref[...]
    for start in range(0, columns, PROJ_STEP):
        stop = min(start + PROJ_STEP, columns)
        done = jnp.dot(
            flattened,
            proj_ref[:, LEFT_COLUMNS + start : LEFT_COLUMNS + stop],
            preferred_element_type=jnp.float32,
        ).astype(jnp.bfloat16)
        done = done.reshape(2, z_size, rows_here, stop - start)
        own_ref[:, :, start:stop] = done[0]
        send_ref[:, :, start:stop] = done[1]


def make_values(owned_latents, value_up, output_proj, owners, rows_here):
    owned, lat, value_size = value_up.shape
    depth, width = output_proj.shape
    columns = width - LEFT_COLUMNS
    rows = owners * rows_here
    vmem = pl.BlockSpec(memory_space=pltpu.VMEM)
    half = jax.ShapeDtypeStruct((owners // 2, rows_here, columns), jnp.bfloat16)
    return pl.pallas_call(
        values_kernel,
        out_shape=(jax.ShapeDtypeStruct((rows, owned * value_size), jnp.bfloat16), half, half),
        in_specs=[[vmem] * owners, vmem, vmem],
        out_specs=(vmem, vmem, vmem),
        scratch_shapes=[pltpu.VMEM((lat // 128, rows * owned, 128), jnp.float32)],
        cost_estimate=pl.CostEstimate(
            flops=2 * rows * depth * columns, bytes_accessed=2 * depth * columns, transcendentals=0
        ),
        compiler_params=pltpu.CompilerParams(vmem_limit_bytes=20 * MIB),
        name="values",
    )(owned_latents, value_up, pltpu.with_memory_space_constraint(output_proj, pltpu.VMEM))


def project_kernel(values_ref, proj_ref, *out_refs):
    rows_here, columns = out_refs[0].shape[1:]
    z_size = len(out_refs)
    flattened = values_ref[...]
    for start in range(0, columns, PROJ_STEP):
        stop = min(start + PROJ_STEP, columns)
        done = jnp.dot(
            flattened, proj_ref[:, start:stop], preferred_element_type=jnp.float32
        ).astype(jnp.bfloat16)
        done = done.reshape(2, z_size, rows_here, stop - start)
        for step in range(z_size):
            out_refs[step][:, :, start:stop] = done[:, step]


def project(values, output_proj, owners, rows_here):
    rows, depth = values.shape
    columns = LEFT_COLUMNS
    z_size = owners // 2
    vmem = pl.BlockSpec(memory_space=pltpu.VMEM)
    part = jax.ShapeDtypeStruct((2, rows_here, columns), jnp.bfloat16)
    return pl.pallas_call(
        project_kernel,
        out_shape=[part] * z_size,
        in_specs=[vmem, vmem],
        out_specs=[vmem] * z_size,
        cost_estimate=pl.CostEstimate(
            flops=2 * rows * depth * columns, bytes_accessed=2 * depth * columns, transcendentals=0
        ),
        compiler_params=pltpu.CompilerParams(vmem_limit_bytes=20 * MIB),
        name="project",
    )(values, pltpu.with_memory_space_constraint(output_proj, pltpu.VMEM))


def add_far_kernel(own_ref, came_ref, *out_refs):
    for step, out_ref in enumerate(out_refs, 1):
        both = own_ref[step].astype(jnp.float32) + came_ref[step].astype(jnp.float32)
        out_ref[...] = both.astype(jnp.bfloat16)


def add_far(own, came):
    vmem = pl.BlockSpec(memory_space=pltpu.VMEM)
    return pl.pallas_call(
        add_far_kernel,
        out_shape=[jax.ShapeDtypeStruct(own.shape[1:], jnp.bfloat16)] * (own.shape[0] - 1),
        in_specs=[vmem, vmem],
        out_specs=[vmem] * (own.shape[0] - 1),
        cost_estimate=pl.CostEstimate(flops=own.size, bytes_accessed=own.size * 6, transcendentals=0),
        compiler_params=pltpu.CompilerParams(vmem_limit_bytes=16 * MIB),
        name="add_far",
    )(own, came)


def add_near_kernel(*refs):
    *part_refs, out_ref = refs
    total = part_refs[0][1].astype(jnp.float32)
    for part_ref in part_refs[1:]:
        total = total + part_ref[1].astype(jnp.float32)
    out_ref[...] = total.astype(jnp.bfloat16)


def add_near(parts):
    vmem = pl.BlockSpec(memory_space=pltpu.VMEM)
    return pl.pallas_call(
        add_near_kernel,
        out_shape=jax.ShapeDtypeStruct(parts[0].shape[1:], jnp.bfloat16),
        in_specs=[vmem] * len(parts),
        out_specs=vmem,
        cost_estimate=pl.CostEstimate(
            flops=parts[0].size * 2, bytes_accessed=parts[0].size * 8, transcendentals=0
        ),
        compiler_params=pltpu.CompilerParams(vmem_limit_bytes=16 * MIB),
        name="add_near",
    )(*parts)


def finish_kernel(near_refs, far_ref, own_ref, came_ref, step_refs, residual_ref, gain_ref,
                  hidden_ref, normed_ref):
    rows, first = far_ref.shape
    width = residual_ref.shape[1]
    left = residual_ref[:, :first].astype(jnp.float32) + far_ref[...].astype(jnp.float32)
    for near_ref in near_refs:
        left = left + near_ref[0].astype(jnp.float32)
    right = residual_ref[:, first:].astype(jnp.float32) + (
        own_ref[0].astype(jnp.float32) + came_ref[0].astype(jnp.float32)
    )
    for step_ref in step_refs:
        right = right + step_ref[...].astype(jnp.float32)
    total = jnp.sum(left * left, axis=1, keepdims=True) + jnp.sum(
        right * right, axis=1, keepdims=True
    )
    inverse_rms = lax.rsqrt(total * (1.0 / width) + norm_eps)
    for part, here in ((left, slice(0, first)), (right, slice(first, width))):
        hidden_ref[:, here] = part.astype(jnp.bfloat16)
        normed = part * inverse_rms * gain_ref[:, here].astype(jnp.float32)
        normed_ref[:, here] = normed.astype(jnp.bfloat16)


def finish(nears, far, own, came, steps, residual, norm_gain):
    vmem = pl.BlockSpec(memory_space=pltpu.VMEM)
    shape = jax.ShapeDtypeStruct(residual.shape, jnp.bfloat16)
    return pl.pallas_call(
        finish_kernel,
        out_shape=(shape, shape),
        in_specs=[[vmem] * len(nears), vmem, vmem, vmem, [vmem] * len(steps), vmem, vmem],
        out_specs=(vmem, vmem),
        compiler_params=pltpu.CompilerParams(vmem_limit_bytes=32 * MIB),
        name="finish",
    )(nears, far, own, came, steps, residual, norm_gain.reshape(1, -1))


def send(array, places, mesh_shape):
    replicas, owners = mesh_shape
    z_size = owners // 2
    pairs = []
    for replica in range(replicas):
        far, step = divmod(places[replica % 2], z_size)
        step = -step if replica % 2 else step
        for owner in range(owners):
            to_replica = (replica + far * (replicas // 2)) % replicas
            to_half = (owner // z_size + far) % 2
            to_owner = to_half * z_size + (owner + step) % z_size
            pairs.append((replica * owners + owner, to_replica * owners + to_owner))
    return lax.ppermute(array, ("rep", "dp"), pairs)


def per_device(
    queries, latent_cache, new_latent, lengths, value_up, output_proj, residual, norm_gain
):
    owners = lax.axis_size("dp")
    mesh_shape = (lax.axis_size("rep"), owners)
    rows_here = latent_cache.shape[0]
    z_size = owners // 2
    latents = attend(queries, latent_cache, new_latent, lengths, owners)
    owned_latents = [latents[0]] + [
        send(latent, places, mesh_shape) for latent, places in zip(latents[1:], zip(*ORDERS))
    ]
    proj_near = bring(output_proj, latents[0])
    values, own, across = make_values(owned_latents, value_up, proj_near, owners, rows_here)
    came = send(across, (z_size, z_size), mesh_shape)
    parts = project(values, proj_near, owners, rows_here)
    nears = [parts[0]] + [send(parts[k], (k, k), mesh_shape) for k in Z_ORDER]
    pairs = add_far(own, came)
    steps = [send(pairs[k - 1], (k, k), mesh_shape) for k in Z_ORDER]
    far = send(add_near(nears), (z_size, z_size), mesh_shape)
    return finish(nears, far, own, came, steps, residual, norm_gain)


def solution(mesh):
    return jax.shard_map(
        per_device,
        mesh=mesh,
        in_specs=(
            P(("rep", "dp"), None, None),
            P(("rep", "dp"), None, None),
            P(("rep", "dp"), None),
            P("rep"),
            P("dp", None, None),
            P("dp", None),
            P(("rep", "dp"), None),
            P(),
        ),
        out_specs=(P(("rep", "dp"), None), P(("rep", "dp"), None)),
        check_vma=False,
    )
```

```python
import jax
import jax.numpy as jnp
from jax import lax
from jax.experimental import pallas as pl
from jax.experimental.pallas import tpu as pltpu
from jax.sharding import PartitionSpec as P

LAT = 512
GROUP_ROWS = 4
PROJ_STEP = 1024
LEFT_COLUMNS = 3456
ORDERS = ((6, 5, 7, 4, 2, 1, 3), (6, 5, 7, 4, 2, 1, 3))
exponent_scale = 192.0 ** (-0.5) * 1.4426950408889634
norm_eps = 1e-06
MIB = 1024 * 1024


def attend_kernel(
    lengths_hbm, queries_hbm, latent_hbm, cache_hbm, *refs
):
    *owner_refs, out_ref = refs[:-9]
    (
        held, queries_ref, latent_ref, latent_wide,
        lengths_ref, order, arrived_small, arrived_queries, arrived_keys,
    ) = refs[-9:]
    row_count, width, span = held.shape
    owners, _, _ = out_ref.shape
    heads = queries_ref.shape[1]
    owned = heads // owners
    first_row = lax.axis_index("dp") * row_count
    pair_count = row_count // 2
    group_pairs = GROUP_ROWS // 2
    group_count = pair_count // group_pairs
    short = span // 2

    lengths_copy = pltpu.make_async_copy(lengths_hbm, lengths_ref, arrived_small.at[0])
    latent_copy = pltpu.make_async_copy(latent_hbm, latent_ref, arrived_small.at[1])

    def fetch_queries(pair):
        rows = pl.ds(2 * pair, 2)
        return pltpu.make_async_copy(
            queries_hbm.at[rows], queries_ref.at[rows], arrived_queries.at[pair]
        )

    def fetch_keys(pair, keys):
        rows = pl.ds(2 * pair, 2)
        return pltpu.make_async_copy(
            cache_hbm.at[rows, :, pl.ds(0, keys)],
            held.at[rows, :, pl.ds(0, keys)],
            arrived_keys.at[pair],
        )

    for pair in range(group_pairs):
        order[pair] = pair
        fetch_queries(pair).start()
        fetch_keys(pair, span).start()
    lengths_copy.start()
    latent_copy.start()
    lengths_copy.wait()
    longest = [
        jnp.maximum(lengths_ref[first_row + 2 * pair], lengths_ref[first_row + 2 * pair + 1])
        for pair in range(pair_count)
    ]
    is_long = [(length > short).astype(jnp.int32) for length in longest]

    short_slot = group_pairs
    long_slot = pair_count - sum(is_long[group_pairs:])
    first_is_long = sum(is_long[:group_pairs]) > 0
    short_groups = long_slot // group_pairs
    for pair in range(group_pairs, pair_count):
        order[jnp.where(is_long[pair] == 1, long_slot, short_slot)] = pair
        long_slot = long_slot + is_long[pair]
        short_slot = short_slot + 1 - is_long[pair]

    def start(group):
        for pair in [order[group * group_pairs + i] for i in range(group_pairs)]:
            fetch_queries(pair).start()

            @pl.when(group < short_groups)
            def _():
                fetch_keys(pair, short).start()

            @pl.when(group >= short_groups)
            def _():
                fetch_keys(pair, span).start()

    start(1)
    start(2)
    latent_copy.wait()
    latent_wide[...] = latent_ref[...].astype(jnp.float32)

    def score(row, keys):
        scores = jnp.dot(
            queries_ref[row], held[row, :, :keys], preferred_element_type=jnp.float32
        )
        position = lax.broadcasted_iota(jnp.int32, scores.shape, 1)
        return jnp.where(position < lengths_ref[first_row + row], scores, -jnp.inf)

    def weigh(row, scores):
        fresh = latent_wide[pl.ds(row, 1), :]
        self_score = jnp.sum(
            queries_ref[row].astype(jnp.float32) * fresh, axis=1, keepdims=True
        )
        row_max = jnp.maximum(jnp.max(scores, axis=1, keepdims=True), self_score)
        raised = jnp.exp2((scores - row_max) * exponent_scale)
        self_raised = jnp.exp2((self_score - row_max) * exponent_scale)
        row_total = jnp.sum(raised, axis=1, keepdims=True) + self_raised
        self_weight = self_raised.astype(jnp.bfloat16).astype(jnp.float32)
        return raised.astype(jnp.bfloat16), self_weight, row_total

    def gather(row, keys, weights, self_weight, row_total):
        gathered = lax.dot_general(
            weights,
            held[row, :LAT, :keys],
            (((1,), (1,)), ((), ())),
            preferred_element_type=jnp.float32,
        )
        gathered = gathered + self_weight * latent_wide[pl.ds(row, 1), :LAT]
        return (gathered * (1.0 / row_total)).reshape(owners, owned, LAT)

    def attend_rows(pairs, keys):
        rows = [2 * pair + i for pair in pairs for i in range(2)]
        scored = [score(row, keys) for row in rows]
        weighed = [weigh(row, scores) for row, scores in zip(rows, scored)]
        done = [gather(row, keys, *parts) for row, parts in zip(rows, weighed)]
        size = 2 * owned
        for i, pair in enumerate(pairs):
            out_ref[:, pl.ds(pl.multiple_of(pair * size, size), size), :] = jnp.concatenate(
                done[2 * i : 2 * i + 2], axis=1
            ).astype(jnp.bfloat16)

    def attend_group(group, carry):
        pairs = [order[group * group_pairs + i] for i in range(group_pairs)]
        whole = jnp.logical_or(group == 0, group >= short_groups)
        is_long = jnp.where(group == 0, first_is_long, group >= short_groups)
        for pair in pairs:
            fetch_queries(pair).wait()

            @pl.when(whole)
            def _():
                fetch_keys(pair, span).wait()

            @pl.when(jnp.logical_not(whole))
            def _():
                fetch_keys(pair, short).wait()

        @pl.when(group == 0)
        def _():
            for later in range(3, group_count):
                start(later)

        @pl.when(is_long)
        def _():
            attend_rows(pairs, span)

        @pl.when(jnp.logical_not(is_long))
        def _():
            attend_rows(pairs, short)

        return carry

    lax.fori_loop(0, group_count, attend_group, 0)
    here = lax.axis_index("dp")
    core = lax.axis_index("rep") % 2
    z_size = owners // 2
    for owner_ref, places in zip(owner_refs, ((0, 0),) + tuple(zip(*ORDERS))):
        place = jnp.where(core == 0, *places)
        far = (here // z_size + place // z_size) % 2
        step = jnp.where(core == 0, place, z_size - place % z_size)
        owner_ref[...] = out_ref[far * z_size + (here + step) % z_size]


def attend(queries, latent_cache, new_latent, lengths, owners):
    row_count, span, width = latent_cache.shape
    heads = queries.shape[1]
    owned = heads // owners
    vmem = pl.BlockSpec(memory_space=pltpu.VMEM)
    hbm = pl.BlockSpec(memory_space=pltpu.HBM)
    arrays = (lengths, queries, new_latent, jnp.swapaxes(latent_cache, 1, 2))
    return pl.pallas_call(
        attend_kernel,
        out_shape=[jax.ShapeDtypeStruct((row_count * owned, LAT), jnp.bfloat16)] * owners,
        in_specs=[hbm] * len(arrays),
        out_specs=[vmem] * owners,
        scratch_shapes=[
            pltpu.VMEM((owners, row_count * owned, LAT), jnp.bfloat16),
            pltpu.VMEM((row_count, width, span), jnp.bfloat16),
            pltpu.VMEM(queries.shape, jnp.bfloat16),
            pltpu.VMEM(new_latent.shape, jnp.bfloat16),
            pltpu.VMEM(new_latent.shape, jnp.float32),
            pltpu.SMEM(lengths.shape, jnp.int32),
            pltpu.SMEM((row_count // 2,), jnp.int32),
            pltpu.SemaphoreType.DMA((2,)),
            pltpu.SemaphoreType.DMA((row_count // 2,)),
            pltpu.SemaphoreType.DMA((row_count // 2,)),
        ],
        cost_estimate=pl.CostEstimate(
            flops=4 * row_count * heads * span * width,
            bytes_accessed=2 * row_count * span * width,
            transcendentals=row_count * heads * span,
        ),
        compiler_params=pltpu.CompilerParams(vmem_limit_bytes=24 * MIB),
        name="attend",
    )(*(pltpu.with_memory_space_constraint(x, pltpu.HBM) for x in arrays))


def bring_kernel(after_hbm, proj_hbm, proj_ref, arrived):
    del after_hbm
    copy = pltpu.make_async_copy(proj_hbm, proj_ref, arrived)
    copy.start()
    copy.wait()


def bring(output_proj, after):
    return pl.pallas_call(
        bring_kernel,
        out_shape=pltpu.VMEM(output_proj.shape, jnp.bfloat16),
        in_specs=[pl.BlockSpec(memory_space=pl.ANY), pl.BlockSpec(memory_space=pltpu.HBM)],
        out_specs=pl.BlockSpec(memory_space=pltpu.VMEM),
        scratch_shapes=[pltpu.SemaphoreType.DMA],
        cost_estimate=pl.CostEstimate(
            flops=0, bytes_accessed=2 * output_proj.size, transcendentals=0
        ),
        compiler_params=pltpu.CompilerParams(vmem_limit_bytes=16 * MIB),
        name="bring",
    )(after, pltpu.with_memory_space_constraint(output_proj, pltpu.HBM))


def values_kernel(latent_refs, value_up_ref, proj_ref, values_ref, own_ref, send_ref, wide):
    owned, lat, value_size = value_up_ref.shape
    owners, rows_here, columns = 2 * own_ref.shape[0], own_ref.shape[1], own_ref.shape[2]
    rows = owners * rows_here
    z_size = owners // 2

    size = rows_here * owned
    core = lax.axis_index("rep") % 2
    for latent_ref, places in zip(latent_refs, ((0, 0),) + tuple(zip(*ORDERS))):
        place = jnp.where(core == 0, *places)
        step = (z_size - place % z_size) % z_size
        back = pl.multiple_of((place // z_size * z_size + step) * size, size)
        for c in range(lat // 128):
            wide[c, pl.ds(back, size)] = latent_ref[:, c * 128 : (c + 1) * 128].astype(
                jnp.float32
            )
    for h in range(owned):
        mine = jnp.concatenate(
            [wide[c, pl.ds(h, rows, stride=owned), :] for c in range(lat // 128)], axis=1
        ).astype(jnp.bfloat16)
        values_ref[:, h * value_size : (h + 1) * value_size] = jnp.dot(
            mine, value_up_ref[h], preferred_element_type=jnp.float32
        ).astype(jnp.bfloat16)
    flattened = values_ref[...]
    for start in range(0, columns, PROJ_STEP):
        stop = min(start + PROJ_STEP, columns)
        done = jnp.dot(
            flattened,
            proj_ref[:, LEFT_COLUMNS + start : LEFT_COLUMNS + stop],
            preferred_element_type=jnp.float32,
        ).astype(jnp.bfloat16)
        done = done.reshape(2, z_size, rows_here, stop - start)
        own_ref[:, :, start:stop] = done[0]
        send_ref[:, :, start:stop] = done[1]


def make_values(owned_latents, value_up, output_proj, owners, rows_here):
    owned, lat, value_size = value_up.shape
    depth, width = output_proj.shape
    columns = width - LEFT_COLUMNS
    rows = owners * rows_here
    vmem = pl.BlockSpec(memory_space=pltpu.VMEM)
    half = jax.ShapeDtypeStruct((owners // 2, rows_here, columns), jnp.bfloat16)
    return pl.pallas_call(
        values_kernel,
        out_shape=(jax.ShapeDtypeStruct((rows, owned * value_size), jnp.bfloat16), half, half),
        in_specs=[[vmem] * owners, vmem, vmem],
        out_specs=(vmem, vmem, vmem),
        scratch_shapes=[pltpu.VMEM((lat // 128, rows * owned, 128), jnp.float32)],
        cost_estimate=pl.CostEstimate(
            flops=2 * rows * depth * columns, bytes_accessed=2 * depth * columns, transcendentals=0
        ),
        compiler_params=pltpu.CompilerParams(vmem_limit_bytes=20 * MIB),
        name="values",
    )(owned_latents, value_up, pltpu.with_memory_space_constraint(output_proj, pltpu.VMEM))


def project_kernel(values_ref, proj_ref, *out_refs):
    rows_here, columns = out_refs[0].shape[1:]
    z_size = len(out_refs)
    flattened = values_ref[...]
    for start in range(0, columns, PROJ_STEP):
        stop = min(start + PROJ_STEP, columns)
        done = jnp.dot(
            flattened, proj_ref[:, start:stop], preferred_element_type=jnp.float32
        ).astype(jnp.bfloat16)
        done = done.reshape(2, z_size, rows_here, stop - start)
        for step in range(z_size):
            out_refs[step][:, :, start:stop] = done[:, step]


def project(values, output_proj, owners, rows_here):
    rows, depth = values.shape
    columns = LEFT_COLUMNS
    z_size = owners // 2
    vmem = pl.BlockSpec(memory_space=pltpu.VMEM)
    part = jax.ShapeDtypeStruct((2, rows_here, columns), jnp.bfloat16)
    return pl.pallas_call(
        project_kernel,
        out_shape=[part] * z_size,
        in_specs=[vmem, vmem],
        out_specs=[vmem] * z_size,
        cost_estimate=pl.CostEstimate(
            flops=2 * rows * depth * columns, bytes_accessed=2 * depth * columns, transcendentals=0
        ),
        compiler_params=pltpu.CompilerParams(vmem_limit_bytes=20 * MIB),
        name="project",
    )(values, pltpu.with_memory_space_constraint(output_proj, pltpu.VMEM))


def add_far_kernel(own_ref, came_ref, *out_refs):
    for step, out_ref in enumerate(out_refs, 1):
        both = own_ref[step].astype(jnp.float32) + came_ref[step].astype(jnp.float32)
        out_ref[...] = both.astype(jnp.bfloat16)


def add_far(own, came):
    vmem = pl.BlockSpec(memory_space=pltpu.VMEM)
    return pl.pallas_call(
        add_far_kernel,
        out_shape=[jax.ShapeDtypeStruct(own.shape[1:], jnp.bfloat16)] * (own.shape[0] - 1),
        in_specs=[vmem, vmem],
        out_specs=[vmem] * (own.shape[0] - 1),
        cost_estimate=pl.CostEstimate(flops=own.size, bytes_accessed=own.size * 6, transcendentals=0),
        compiler_params=pltpu.CompilerParams(vmem_limit_bytes=16 * MIB),
        name="add_far",
    )(own, came)


def add_near_kernel(*refs):
    *part_refs, out_ref = refs
    total = part_refs[0][1].astype(jnp.float32)
    for part_ref in part_refs[1:]:
        total = total + part_ref[1].astype(jnp.float32)
    out_ref[...] = total.astype(jnp.bfloat16)


def add_near(parts):
    vmem = pl.BlockSpec(memory_space=pltpu.VMEM)
    return pl.pallas_call(
        add_near_kernel,
        out_shape=jax.ShapeDtypeStruct(parts[0].shape[1:], jnp.bfloat16),
        in_specs=[vmem] * len(parts),
        out_specs=vmem,
        cost_estimate=pl.CostEstimate(
            flops=parts[0].size * 2, bytes_accessed=parts[0].size * 8, transcendentals=0
        ),
        compiler_params=pltpu.CompilerParams(vmem_limit_bytes=16 * MIB),
        name="add_near",
    )(*parts)


def finish_kernel(near_refs, far_ref, own_ref, came_ref, step_refs, residual_ref, gain_ref,
                  hidden_ref, normed_ref):
    rows, first = far_ref.shape
    width = residual_ref.shape[1]
    left = residual_ref[:, :first].astype(jnp.float32) + far_ref[...].astype(jnp.float32)
    for near_ref in near_refs:
        left = left + near_ref[0].astype(jnp.float32)
    right = residual_ref[:, first:].astype(jnp.float32) + (
        own_ref[0].astype(jnp.float32) + came_ref[0].astype(jnp.float32)
    )
    for step_ref in step_refs:
        right = right + step_ref[...].astype(jnp.float32)
    total = jnp.sum(left * left, axis=1, keepdims=True) + jnp.sum(
        right * right, axis=1, keepdims=True
    )
    inverse_rms = lax.rsqrt(total * (1.0 / width) + norm_eps)
    for part, here in ((left, slice(0, first)), (right, slice(first, width))):
        hidden_ref[:, here] = part.astype(jnp.bfloat16)
        normed = part * inverse_rms * gain_ref[:, here].astype(jnp.float32)
        normed_ref[:, here] = normed.astype(jnp.bfloat16)


def finish(nears, far, own, came, steps, residual, norm_gain):
    vmem = pl.BlockSpec(memory_space=pltpu.VMEM)
    shape = jax.ShapeDtypeStruct(residual.shape, jnp.bfloat16)
    return pl.pallas_call(
        finish_kernel,
        out_shape=(shape, shape),
        in_specs=[[vmem] * len(nears), vmem, vmem, vmem, [vmem] * len(steps), vmem, vmem],
        out_specs=(vmem, vmem),
        compiler_params=pltpu.CompilerParams(vmem_limit_bytes=32 * MIB),
        name="finish",
    )(nears, far, own, came, steps, residual, norm_gain.reshape(1, -1))


def send(array, places, mesh_shape):
    replicas, owners = mesh_shape
    z_size = owners // 2
    pairs = []
    for replica in range(replicas):
        far, step = divmod(places[replica % 2], z_size)
        step = -step if replica % 2 else step
        for owner in range(owners):
            to_replica = (replica + far * (replicas // 2)) % replicas
            to_half = (owner // z_size + far) % 2
            to_owner = to_half * z_size + (owner + step) % z_size
            pairs.append((replica * owners + owner, to_replica * owners + to_owner))
    return lax.ppermute(array, ("rep", "dp"), pairs)


def per_device(
    queries, latent_cache, new_latent, lengths, value_up, output_proj, residual, norm_gain
):
    owners = lax.axis_size("dp")
    mesh_shape = (lax.axis_size("rep"), owners)
    rows_here = latent_cache.shape[0]
    z_size = owners // 2
    latents = attend(queries, latent_cache, new_latent, lengths, owners)
    owned_latents = [latents[0]] + [
        send(latent, places, mesh_shape) for latent, places in zip(latents[1:], zip(*ORDERS))
    ]
    proj_near = bring(output_proj, latents[0])
    values, own, across = make_values(owned_latents, value_up, proj_near, owners, rows_here)
    came = send(across, (z_size, z_size), mesh_shape)
    parts = project(values, proj_near, owners, rows_here)
    nears = [parts[0]] + [send(parts[k], (k, k), mesh_shape) for k in range(1, z_size)]
    pairs = add_far(own, came)
    steps = [send(pair, (k, k), mesh_shape) for k, pair in enumerate(pairs, 1)]
    far = send(add_near(nears), (z_size, z_size), mesh_shape)
    return finish(nears, far, own, came, steps, residual, norm_gain)


def solution(mesh):
    return jax.shard_map(
        per_device,
        mesh=mesh,
        in_specs=(
            P(("rep", "dp"), None, None),
            P(("rep", "dp"), None, None),
            P(("rep", "dp"), None),
            P("rep"),
            P("dp", None, None),
            P("dp", None),
            P(("rep", "dp"), None),
            P(),
        ),
        out_specs=(P(("rep", "dp"), None), P(("rep", "dp"), None)),
        check_vma=False,
    )
```
